32 devices in a mesh: dp: 16 (over z, y, core), tensor: 2 (over x).
Axes of the slice: x: 2, y: 2, z: 4, core: 2. Of those that a mesh axis runs over, the one named last changes fastest.
Arguments:
- tokens: bfloat16 [1024, 32, 1024], P('tensor', 'dp'), may hold values from -6 to 6
- d_out: bfloat16 [1024, 32, 1024], P('tensor', 'dp'), may hold values from -6 to 6
- ln1_gain: bfloat16 [1024], P('dp'), may hold values from 0.099609375 to 1.8984375
- ln1_bias: bfloat16 [1024], P('dp'), may hold values from -1.75 to 1.75
- w_qkv: bfloat16 [3, 1024, 1024], P(None, 'dp', 'tensor'), may hold values from -0.1875 to 0.1875
- w_out: bfloat16 [1024, 1024], P('tensor', 'dp'), may hold values from -3 to 3
- ln2_gain: bfloat16 [1024], P('dp'), may hold values from 0.099609375 to 1.8984375
- ln2_bias: bfloat16 [1024], P('dp'), may hold values from -1.75 to 1.75
- w_up: bfloat16 [1024, 4096], P('dp', 'tensor'), may hold values from -0.1875 to 0.1875
- w_down: bfloat16 [4096, 1024], P('tensor', 'dp'), may hold values from -0.09375 to 0.09375
Outputs:
- block_out: bfloat16 [1024, 32, 1024], P('tensor', 'dp')
- input_grad: bfloat16 [1024, 32, 1024], P('tensor', 'dp')
- grad_ln1_gain: float32 [1024], P('dp')
- grad_ln1_bias: float32 [1024], P('dp')
- grad_w_qkv: float32 [3, 1024, 1024], P(None, 'dp', 'tensor')
- grad_w_out: float32 [1024, 1024], P('tensor', 'dp')
- grad_ln2_gain: float32 [1024], P('dp')
- grad_ln2_bias: float32 [1024], P('dp')
- grad_w_up: float32 [1024, 4096], P('dp', 'tensor')
- grad_w_down: float32 [4096, 1024], P('tensor', 'dp')
The draws below stay inside these ranges and needn't reach their ends.
All inputs are finite; a program needn't handle non-finite values.
Results may differ from the reference program's by a relative error of at most 0.023.
Values may be sent and summed in bfloat16 or wider, within the bound.
No kernel may reach another device: no remote copies, remote signals or barrier semaphores. Data moves between devices by JAX's collectives and lax.ppermute only.
A program may use at most 256 MiB of HBM per device.

```python
import jax
import jax.numpy as jnp
from jax import lax

D = 1024
HEADS = 16
HEAD_DIM = 64
FF = 4096
SEQ_LEN = 1024
SEQ_DEV = 2
SEQS = 32


def block_scale(key, extent, pieces, low, top_value):
    gain = 1.0
    for dim, blocks in pieces:
        heights = jax.random.uniform(jax.random.fold_in(jax.random.fold_in(key, 6), dim), (blocks,), jnp.float32, low / len(pieces), top_value / len(pieces))
        gain = gain * jnp.repeat(jnp.exp(heights), extent[dim] // blocks).reshape((-1,) + (1,) * (len(extent) - 1 - dim))
    return gain


def noise(stream_key, shape, scale, reach, cuts=(), kind=jnp.bfloat16):
    array = jax.random.normal(stream_key, shape, jnp.float32) * scale
    if len(cuts) > 0:
        array = block_scale(stream_key, shape, cuts, -0.22, 0.18) * array
    return jnp.clip(array, min=-reach, max=reach).astype(kind)


def setup_inputs(seed: int = 0) -> dict:
    seeds = jax.random.split(jax.random.key(seed), 11)
    tokens = noise(seeds[0], (SEQ_LEN, SEQS, D), 1.0, 6.0, ((0, 2), (1, 16)))
    d_out = noise(seeds[1], (SEQ_LEN, SEQS, D), 1.0, 6.0, ((0, 2), (1, 16)))
    ln1_gain = jnp.clip(1.0 + 0.18 * jax.random.normal(seeds[2], (D,), jnp.float32), 0.099609375, 1.8984375).astype(jnp.bfloat16)
    ln1_bias = noise(seeds[3], (D,), 0.3, 1.75, ((0, 16),))
    w_qkv = noise(seeds[4], (3, D, D), D ** -0.5, 0.1875, ((1, 16), (2, 2)))
    w_out = noise(seeds[5], (D, D), (D * 4 // SEQ_LEN) ** -0.5, 3.0, ((0, 2), (1, 16)))
    ln2_gain = jnp.clip(1.0 + 0.18 * jax.random.normal(seeds[6], (D,), jnp.float32), 0.099609375, 1.8984375).astype(jnp.bfloat16)
    ln2_bias = noise(seeds[7], (D,), 0.3, 1.75, ((0, 16),))
    w_up = noise(seeds[8], (D, FF), D ** -0.5, 0.1875, ((0, 16), (1, 2)))
    w_down = noise(seeds[9], (FF, D), FF ** -0.5, 0.09375, ((0, 2), (1, 16)))
    return dict(tokens=tokens, d_out=d_out, ln1_gain=ln1_gain, ln1_bias=ln1_bias, w_qkv=w_qkv, w_out=w_out, ln2_gain=ln2_gain, ln2_bias=ln2_bias, w_up=w_up, w_down=w_down)


EPSILON = 1e-05
HIGHEST = lax.Precision.HIGHEST

@jax.custom_vjp
def low(v):
    return lax.optimization_barrier(v.astype(jnp.bfloat16)).astype(jnp.float32)

@jax.custom_vjp
def low_back(v):
    return v

def low_keep(v):
    return (low(v), None)

def low_pass(kept, grad):
    return (grad,)

def back_keep(v):
    return (v, None)

def back_low(kept, grad):
    return (low(grad),)
low.defvjp(low_keep, low_pass)
low_back.defvjp(back_keep, back_low)

def layer_norm(values, norm_gain, norm_bias):
    center = lax.optimization_barrier(jnp.mean(values, axis=-1, keepdims=True))
    centered = values - center
    spread = lax.optimization_barrier(jnp.mean(centered * centered, axis=-1, keepdims=True))
    return centered * lax.rsqrt(spread + EPSILON) * norm_gain + norm_bias

def attend(triple):
    queries, key_rows, value_rows = triple
    length = queries.shape[1]
    scores = jnp.einsum('hqd,hkd->hqk', queries, key_rows, precision=HIGHEST) * HEAD_DIM ** (-0.5)
    scores = low_back(scores)
    row_index = lax.broadcasted_iota(jnp.int32, (length, length), 0)
    column_index = lax.broadcasted_iota(jnp.int32, (length, length), 1)
    scores = jnp.where(column_index <= row_index, scores, -1e+30)
    row_max = lax.optimization_barrier(jnp.max(scores, axis=-1, keepdims=True))
    weights = jnp.exp(scores - row_max)
    shares = low(weights / lax.optimization_barrier(jnp.sum(weights, axis=-1, keepdims=True)))
    return jnp.einsum('hqk,hkd->hqd', shares, value_rows, precision=HIGHEST)

def forward(inputs, ln1_gain, ln1_bias, w_qkv, w_out, ln2_gain, ln2_bias, w_up, w_down):
    groups, length, width = inputs.shape
    normed = low(layer_norm(inputs, ln1_gain, ln1_bias))
    projected = jnp.einsum('gtd,cde->cgte', normed, w_qkv, precision=HIGHEST)
    projected = low_back(low(projected))
    split_heads = projected.reshape(3, groups, length, HEADS, HEAD_DIM).transpose(0, 1, 3, 2, 4)
    mixed = lax.map(jax.checkpoint(attend), (split_heads[0], split_heads[1], split_heads[2]))
    mixed = mixed.transpose(0, 2, 1, 3).reshape(groups, length, width)
    mixed = low_back(low(mixed))
    branch = low_back(jnp.einsum('gte,ed->gtd', mixed, w_out, precision=HIGHEST))
    hidden = inputs + branch
    normed_two = low(layer_norm(hidden, ln2_gain, ln2_bias))
    upward = low_back(jnp.einsum('gtd,df->gtf', normed_two, w_up, precision=HIGHEST))
    active = low(jax.nn.gelu(upward, approximate=True))
    return hidden + jnp.einsum('gtf,fd->gtd', active, w_down, precision=HIGHEST)

def reference(tokens, d_out, ln1_gain, ln1_bias, w_qkv, w_out, ln2_gain, ln2_bias, w_up, w_down):
    weights = tuple((member.astype(jnp.float32) for member in (ln1_gain, ln1_bias, w_qkv, w_out, ln2_gain, ln2_bias, w_up, w_down)))
    inputs = tokens.astype(jnp.float32).reshape(SEQ_LEN, -1, SEQ_DEV, D).transpose(1, 2, 0, 3)
    cotangent = d_out.astype(jnp.float32).reshape(SEQ_LEN, -1, SEQ_DEV, D).transpose(1, 2, 0, 3)

    def group_step(summed, group_pair):
        group_in, group_grad = group_pair
        result, pull_back = jax.vjp(forward, group_in, *weights)
        gradients = pull_back(group_grad)
        summed = tuple((earlier + latest for earlier, latest in zip(summed, gradients[1:])))
        return (summed, (result.astype(jnp.bfloat16), gradients[0].astype(jnp.bfloat16)))
    starting = tuple((jnp.zeros_like(member) for member in weights))
    summed, (outputs, in_grads) = lax.scan(group_step, starting, (inputs, cotangent))
    block_out = outputs.transpose(2, 0, 1, 3).reshape(SEQ_LEN, -1, D)
    input_grad = in_grads.transpose(2, 0, 1, 3).reshape(SEQ_LEN, -1, D)
    return (block_out, input_grad, summed[0], summed[1], summed[2], summed[3], summed[4], summed[5], summed[6], summed[7])
```

```python
import functools
import math

import jax
import jax.numpy as jnp
from jax import lax
from jax.experimental import pallas as pl
from jax.experimental.pallas import tpu as pltpu
from jax.sharding import PartitionSpec as P

HEAD_DIM = 64


EPSILON = 1e-05


def norm_rows(values, norm_gain, norm_bias):
    center = jnp.mean(values, axis=-1, keepdims=True)
    centered = values - center
    inverse = lax.rsqrt(jnp.mean(centered * centered, axis=-1, keepdims=True) + EPSILON)
    normal = centered * inverse
    return (normal * norm_gain + norm_bias, normal, inverse)


def norm_back(grad_in, normal, inverse, norm_gain):
    gain_grad = jnp.sum(grad_in * normal, axis=(0, 1))
    bias_grad = jnp.sum(grad_in, axis=(0, 1))
    scaled = grad_in * norm_gain
    first = jnp.mean(scaled, axis=-1, keepdims=True)
    second = jnp.mean(scaled * normal, axis=-1, keepdims=True)
    return (inverse * (scaled - first - normal * second), gain_grad, bias_grad)


def causal_mask(length):
    row_index = lax.broadcasted_iota(jnp.int32, (length, length), 0)
    column_index = lax.broadcasted_iota(jnp.int32, (length, length), 1)
    return column_index <= row_index


def attend_forward(triple):
    queries, key_rows, value_rows = triple
    scores = jnp.einsum(
        "qhd,khd->hqk", queries, key_rows, preferred_element_type=jnp.float32
    ) * HEAD_DIM ** (-0.5)
    scores = jnp.where(causal_mask(queries.shape[0]), scores, -1e30)
    row_max = jnp.max(scores, axis=-1, keepdims=True)
    weights = jnp.exp(scores - row_max)
    totals = jnp.sum(weights, axis=-1, keepdims=True)
    shares = (weights / totals).astype(jnp.bfloat16)
    mixed = jnp.einsum("hqk,khd->qhd", shares, value_rows, preferred_element_type=jnp.float32)
    return (mixed.astype(jnp.bfloat16), row_max + jnp.log(totals))


def attend_back(group):
    queries, key_rows, value_rows, grad_mixed, log_total = group
    factor = HEAD_DIM ** (-0.5)
    scores = (
        jnp.einsum("qhd,khd->hqk", queries, key_rows, preferred_element_type=jnp.float32) * factor
    )
    scores = jnp.where(causal_mask(queries.shape[0]), scores, -1e30)
    shares = jnp.exp(scores - log_total)
    grad_value = jnp.einsum(
        "hqk,qhd->khd", shares.astype(jnp.bfloat16), grad_mixed, preferred_element_type=jnp.float32
    )
    grad_shares = jnp.einsum(
        "qhd,khd->hqk", grad_mixed, value_rows, preferred_element_type=jnp.float32
    )
    inner = jnp.sum(shares * grad_shares, axis=-1, keepdims=True)
    grad_scores = (shares * (grad_shares - inner)).astype(jnp.bfloat16)
    grad_query = (
        jnp.einsum("hqk,khd->qhd", grad_scores, key_rows, preferred_element_type=jnp.float32)
        * factor
    )
    grad_key = (
        jnp.einsum("hqk,qhd->khd", grad_scores, queries, preferred_element_type=jnp.float32)
        * factor
    )
    return jnp.stack([grad_query, grad_key, grad_value]).astype(jnp.bfloat16)


def on_device_shared(tokens, d_out, ln1_gain, ln1_bias, w_qkv, w_out, ln2_gain, ln2_bias, w_up, w_down):
    local_rows, seq_count, width = tokens.shape
    gathered = (
        lax.all_gather(ln1_gain, "dp", axis=0, tiled=True),
        lax.all_gather(ln1_bias, "dp", axis=0, tiled=True),
        lax.all_gather(w_qkv, "dp", axis=1, tiled=True),
        lax.all_gather(w_out, "dp", axis=1, tiled=True),
        lax.all_gather(ln2_gain, "dp", axis=0, tiled=True),
        lax.all_gather(ln2_bias, "dp", axis=0, tiled=True),
        lax.all_gather(w_up, "dp", axis=0, tiled=True),
        lax.all_gather(w_down, "dp", axis=1, tiled=True),
    )
    gain_one, bias_one, qkv_weight, out_weight, gain_two, bias_two, up_weight, down_weight = (
        gathered
    )
    residual = tokens.astype(jnp.float32)
    normed_one, normal_one, inverse_one = norm_rows(
        residual, gain_one.astype(jnp.float32), bias_one.astype(jnp.float32)
    )
    low_one = normed_one.astype(jnp.bfloat16)
    rows_one = lax.all_gather(low_one, "tensor", axis=0, tiled=True)
    full_rows = rows_one.shape[0]
    projected = jnp.einsum(
        "tgd,cde->cgte", rows_one, qkv_weight, preferred_element_type=jnp.float32
    ).astype(jnp.bfloat16)
    local_width = projected.shape[3]
    heads_local = local_width // HEAD_DIM
    split_heads = projected.reshape(3, seq_count, full_rows, heads_local, HEAD_DIM)
    mixed, log_total = lax.map(attend_forward, (split_heads[0], split_heads[1], split_heads[2]))
    mixed = mixed.reshape(seq_count, full_rows, local_width)
    piece_rows = mixed
    hidden = residual + lax.psum_scatter(
        jnp.einsum(
            "gte,ed->tgd", piece_rows, out_weight, preferred_element_type=jnp.float32
        ).astype(jnp.bfloat16),
        "tensor",
        scatter_dimension=0,
        tiled=True,
    ).astype(jnp.float32)
    normed_two, normal_two, inverse_two = norm_rows(
        hidden, gain_two.astype(jnp.float32), bias_two.astype(jnp.float32)
    )
    low_two = normed_two.astype(jnp.bfloat16)
    rows_two = lax.all_gather(low_two, "tensor", axis=0, tiled=True)
    upward = jnp.einsum("tgd,df->tgf", rows_two, up_weight, preferred_element_type=jnp.float32)
    active = jax.nn.gelu(upward, approximate=True).astype(jnp.bfloat16)
    piece_rows = active
    block_sum = lax.psum_scatter(
        jnp.einsum(
            "tgf,fd->tgd", piece_rows, down_weight, preferred_element_type=jnp.float32
        ).astype(jnp.bfloat16),
        "tensor",
        scatter_dimension=0,
        tiled=True,
    ).astype(jnp.float32)
    block_out = (hidden + block_sum).astype(jnp.bfloat16)
    grad_rows = lax.all_gather(d_out, "tensor", axis=0, tiled=True)
    grad_down = jnp.einsum("tgf,tgd->fd", active, grad_rows, preferred_element_type=jnp.float32)
    grad_active = jnp.einsum(
        "tgd,fd->tgf", grad_rows, down_weight, preferred_element_type=jnp.float32
    )
    gelu_pull = jax.vjp(lambda inner: jax.nn.gelu(inner, approximate=True), upward)[1]
    grad_upward = gelu_pull(grad_active)[0].astype(jnp.bfloat16)
    grad_up = jnp.einsum("tgd,tgf->df", rows_two, grad_upward, preferred_element_type=jnp.float32)
    piece_rows = grad_upward
    grad_normed_two = lax.psum_scatter(
        jnp.einsum("tgf,df->tgd", piece_rows, up_weight, preferred_element_type=jnp.float32).astype(
            jnp.bfloat16
        ),
        "tensor",
        scatter_dimension=0,
        tiled=True,
    ).astype(jnp.float32)
    grad_hidden_norm, gain_two_grad, bias_two_grad = norm_back(
        grad_normed_two, normal_two, inverse_two, gain_two.astype(jnp.float32)
    )
    grad_hidden = d_out.astype(jnp.float32) + grad_hidden_norm
    low_hidden = grad_hidden.astype(jnp.bfloat16)
    hidden_rows = lax.all_gather(low_hidden, "tensor", axis=0, tiled=True)
    grad_out = jnp.einsum("gte,tgd->ed", mixed, hidden_rows, preferred_element_type=jnp.float32)
    grad_mixed = jnp.einsum(
        "tgd,ed->gte", hidden_rows, out_weight, preferred_element_type=jnp.float32
    ).astype(jnp.bfloat16)
    grad_heads = lax.map(
        attend_back,
        (
            split_heads[0],
            split_heads[1],
            split_heads[2],
            grad_mixed.reshape(seq_count, full_rows, heads_local, HEAD_DIM),
            log_total,
        ),
    )
    grad_projected = grad_heads.reshape(seq_count, 3, full_rows, local_width)
    grad_qkv = jnp.einsum(
        "tgd,gcte->cde", rows_one, grad_projected, preferred_element_type=jnp.float32
    )
    piece_rows = grad_projected
    grad_normed_one = lax.psum_scatter(
        jnp.einsum(
            "gcte,cde->tgd", piece_rows, qkv_weight, preferred_element_type=jnp.float32
        ).astype(jnp.bfloat16),
        "tensor",
        scatter_dimension=0,
        tiled=True,
    ).astype(jnp.float32)
    grad_input_norm, gain_one_grad, bias_one_grad = norm_back(
        grad_normed_one, normal_one, inverse_one, gain_one.astype(jnp.float32)
    )
    input_grad = (grad_hidden + grad_input_norm).astype(jnp.bfloat16)
    owned = (
        lax.psum_scatter(
            gain_one_grad.astype(jnp.bfloat16), "dp", scatter_dimension=0, tiled=True
        ).astype(jnp.float32),
        lax.psum_scatter(
            bias_one_grad.astype(jnp.bfloat16), "dp", scatter_dimension=0, tiled=True
        ).astype(jnp.float32),
        lax.psum_scatter(
            grad_qkv.astype(jnp.bfloat16), "dp", scatter_dimension=1, tiled=True
        ).astype(jnp.float32),
        lax.psum_scatter(
            grad_out.astype(jnp.bfloat16), "dp", scatter_dimension=1, tiled=True
        ).astype(jnp.float32),
        lax.psum_scatter(
            gain_two_grad.astype(jnp.bfloat16), "dp", scatter_dimension=0, tiled=True
        ).astype(jnp.float32),
        lax.psum_scatter(
            bias_two_grad.astype(jnp.bfloat16), "dp", scatter_dimension=0, tiled=True
        ).astype(jnp.float32),
        lax.psum_scatter(
            grad_up.astype(jnp.bfloat16), "dp", scatter_dimension=0, tiled=True
        ).astype(jnp.float32),
        lax.psum_scatter(
            grad_down.astype(jnp.bfloat16), "dp", scatter_dimension=1, tiled=True
        ).astype(jnp.float32),
    )
    norm_sums = lax.psum((owned[0], owned[1], owned[4], owned[5]), "tensor")
    return (
        block_out,
        input_grad,
        norm_sums[0],
        norm_sums[1],
        owned[2],
        owned[3],
        norm_sums[2],
        norm_sums[3],
        owned[6],
        owned[7],
    )


LOG2E = 1.4426950408889634
BLOCK = 256
NT = (((1,), (1,)), ((), ()))
TN = (((0,), (0,)), ((), ()))
NN = (((1,), (0,)), ((), ()))


def mul(left, right, dims=NN):
    return lax.dot_general(left, right, dims, preferred_element_type=jnp.float32)


def fwd_kernel(q_ref, k_ref, v_ref, o_ref, lse_ref):
    length = q_ref.shape[0]
    scale = LOG2E * HEAD_DIM**-0.5
    block = min(BLOCK, length)
    keep = lax.broadcasted_iota(jnp.int32, (block, block), 1) <= lax.broadcasted_iota(
        jnp.int32, (block, block), 0
    )
    heads = q_ref.shape[1] // HEAD_DIM
    for i in range(length // block):
        rows = slice(i * block, (i + 1) * block)
        outs = []
        for h in range(heads):
            cols = slice(h * HEAD_DIM, (h + 1) * HEAD_DIM)
            q = q_ref[rows, cols]
            diag = jnp.where(keep, mul(q, k_ref[rows, cols], NT), -1e30)
            top = jnp.max(diag, axis=1, keepdims=True)
            if i > 0:
                past = mul(q, k_ref[: i * block, cols], NT)
                top = jnp.maximum(top, jnp.max(past, axis=1, keepdims=True))
            shift = top * scale
            w = jnp.exp2(diag * scale - shift)
            total = jnp.sum(w, axis=1, keepdims=True)
            out = mul(w.astype(jnp.bfloat16), v_ref[rows, cols])
            if i > 0:
                w = jnp.exp2(past * scale - shift)
                total = total + jnp.sum(w, axis=1, keepdims=True)
                out = out + mul(w.astype(jnp.bfloat16), v_ref[: i * block, cols])
            outs.append(out / total)
            lse = shift + jnp.log2(total)
            lse_ref[0, h : h + 1, rows] = jnp.broadcast_to(lse, (block, 128)).T[:1]
        o_ref[rows, :] = jnp.concatenate(outs, axis=1).astype(jnp.bfloat16)


def attend(qkv):
    length, width3 = qkv.shape
    width = width3 // 3
    pairs = width // 128
    return pl.pallas_call(
        fwd_kernel,
        grid=(pairs,),
        in_specs=[
            pl.BlockSpec((length, 128), lambda j: (0, j)),
            pl.BlockSpec((length, 128), lambda j: (0, pairs + j)),
            pl.BlockSpec((length, 128), lambda j: (0, 2 * pairs + j)),
        ],
        out_specs=[
            pl.BlockSpec((length, 128), lambda j: (0, j)),
            pl.BlockSpec((1, 8, length), lambda j: (j, 0, 0)),
        ],
        out_shape=[
            jax.ShapeDtypeStruct((length, width), jnp.bfloat16),
            jax.ShapeDtypeStruct((pairs, 8, length), jnp.float32),
        ],
        compiler_params=pltpu.CompilerParams(vmem_limit_bytes=40 * 2**20),
        cost_estimate=pl.CostEstimate(
            flops=8 * length * length * width, bytes_accessed=8 * length * width, transcendentals=0
        ),
    )(qkv, qkv, qkv)


def back_kernel(q_ref, k_ref, v_ref, do_ref, o_ref, lse_ref, dqkv_ref):
    length = q_ref.shape[0]
    width = dqkv_ref.shape[1] // 3
    factor = HEAD_DIM**-0.5
    scale = LOG2E * factor
    block = min(BLOCK, length)
    keep = lax.broadcasted_iota(jnp.int32, (block, block), 0) <= lax.broadcasted_iota(
        jnp.int32, (block, block), 1
    )
    count = length // block
    heads = q_ref.shape[1] // HEAD_DIM
    col = pl.program_id(0) * 128
    both = do_ref[...].astype(jnp.float32) * o_ref[...].astype(jnp.float32)
    both = both.T
    deltas = [
        jnp.sum(both[h * HEAD_DIM : (h + 1) * HEAD_DIM], axis=0, keepdims=True)
        for h in range(heads)
    ]
    dqs = [[None] * count for _ in range(heads)]
    for j in range(count):
        rows = slice(j * block, (j + 1) * block)
        dks, dvs = [], []
        for h in range(heads):
            cols = slice(h * HEAD_DIM, (h + 1) * HEAD_DIM)
            k, v = k_ref[rows, cols], v_ref[rows, cols]
            q, do = q_ref[j * block :, cols], do_ref[j * block :, cols]
            lse = lse_ref[0, h : h + 1, j * block :]
            w = jnp.exp2(mul(k, q, NT) * scale - lse)
            if j + 1 < count:
                w = jnp.concatenate([jnp.where(keep, w[:, :block], 0.0), w[:, block:]], axis=1)
            else:
                w = jnp.where(keep, w, 0.0)
            ds = (w * (mul(v, do, NT) - deltas[h][:, j * block :])).astype(jnp.bfloat16)
            dvs.append(mul(w.astype(jnp.bfloat16), do))
            dks.append(mul(ds, q) * factor)
            dq = mul(ds, k, TN)
            for i in range(j, count):
                part = dq[(i - j) * block : (i - j + 1) * block]
                dqs[h][i] = part if dqs[h][i] is None else dqs[h][i] + part
        dqkv_ref[rows, pl.ds(pl.multiple_of(width + col, 128), 128)] = jnp.concatenate(
            dks, axis=1
        ).astype(jnp.bfloat16)
        dqkv_ref[rows, pl.ds(pl.multiple_of(2 * width + col, 128), 128)] = jnp.concatenate(
            dvs, axis=1
        ).astype(jnp.bfloat16)
        dqkv_ref[rows, pl.ds(pl.multiple_of(col, 128), 128)] = (
            jnp.concatenate([dqs[h][j] for h in range(heads)], axis=1) * factor
        ).astype(jnp.bfloat16)


def attend_grad(qkv, grad_mixed, mixed, lse):
    length, width3 = qkv.shape
    width = width3 // 3
    pairs = width // 128
    return pl.pallas_call(
        back_kernel,
        grid=(pairs,),
        in_specs=[
            pl.BlockSpec((length, 128), lambda j: (0, j)),
            pl.BlockSpec((length, 128), lambda j: (0, pairs + j)),
            pl.BlockSpec((length, 128), lambda j: (0, 2 * pairs + j)),
            pl.BlockSpec((length, 128), lambda j: (0, j)),
            pl.BlockSpec((length, 128), lambda j: (0, j)),
            pl.BlockSpec((1, 8, length), lambda j: (j, 0, 0)),
        ],
        out_specs=pl.BlockSpec((length, width3), lambda j: (0, 0)),
        out_shape=jax.ShapeDtypeStruct((length, width3), jnp.bfloat16),
        compiler_params=pltpu.CompilerParams(vmem_limit_bytes=40 * 2**20),
        cost_estimate=pl.CostEstimate(
            flops=20 * length * length * width, bytes_accessed=16 * length * width, transcendentals=0
        ),
    )(qkv, qkv, qkv, grad_mixed, mixed, lse)


def swap_dp(array, size, mask):
    return lax.ppermute(array, "dp", [(i, i ^ mask) for i in range(size)])


def swap_tensor(array):
    return lax.ppermute(array, "tensor", [(0, 1), (1, 0)])


def gather_pair(shard, size, tensor_first, axis=0):
    def grow(array, mask):
        return jnp.concatenate([array, swap_dp(array, size, mask)], axis=axis)

    mask = size // 2
    own = shard
    while mask >= 4:
        own = grow(own, mask)
        mask //= 2
    if tensor_first:
        other = swap_tensor(own)
        own, other = grow(own, 2), grow(other, 2)
    else:
        own = grow(own, 2)
        other = swap_tensor(own)
    return grow(own, 1), grow(other, 1)


def add_low(left, right):
    return (left.astype(jnp.float32) + right.astype(jnp.float32)).astype(jnp.bfloat16)


def scatter_pair(rows, own, other, size, tensor_first):
    half = rows.shape[1] // 2

    def core_sum(columns):
        away = mul(rows[:, half:], columns, TN).astype(jnp.bfloat16)
        arrived = swap_dp(away, size, 1)
        return (mul(rows[:, :half], columns, TN) + arrived.astype(jnp.float32)).astype(jnp.bfloat16)

    def fold(array, mask):
        middle = array.shape[0] // 2
        return array[:middle], swap_dp(array[middle:], size, mask)

    own, other = core_sum(own), core_sum(other)
    if tensor_first:
        own = add_low(own, swap_tensor(other))
        own = add_low(*fold(own, 2))
    else:
        own, other = add_low(*fold(own, 2)), add_low(*fold(other, 2))
        own = add_low(own, swap_tensor(other))
    mask = 4
    while mask < size:
        kept, arrived = fold(own, mask)
        mask *= 2
        if mask < size:
            own = add_low(kept, arrived)
        else:
            own = kept.astype(jnp.float32) + arrived.astype(jnp.float32)
    return own


def norm_rows_grad(grad_in, normal, inverse, norm_gain):
    gain_grad = jnp.sum(grad_in * normal, axis=0, keepdims=True)
    bias_grad = jnp.sum(grad_in, axis=0, keepdims=True)
    scaled = grad_in * norm_gain
    first = jnp.mean(scaled, axis=-1, keepdims=True)
    second = jnp.mean(scaled * normal, axis=-1, keepdims=True)
    return (inverse * (scaled - first - normal * second), gain_grad, bias_grad)


def block_order(size, width):
    block = width // size
    here = lax.axis_index("dp")
    column = lax.broadcasted_iota(jnp.int32, (width, width), 1)
    place, inside = column // block, column % block
    source = here
    bit, value = size // 2, 1
    while bit >= 1:
        source = source ^ jnp.where((place // bit) % 2 == 1, value, 0)
        bit //= 2
        value *= 2
    row = lax.broadcasted_iota(jnp.int32, (width, width), 0)
    return (row == source * block + inside).astype(jnp.bfloat16)


def gelu_both(u):
    inner = math.sqrt(2 / math.pi)
    t = jnp.tanh(inner * (u + 0.044715 * u * u * u))
    slope = 0.5 * (1.0 + t) + 0.5 * u * (1.0 - t * t) * inner * (1.0 + 3 * 0.044715 * u * u)
    return 0.5 * u * (1.0 + t), slope


def on_device_whole(
    size, tokens, d_out, ln1_gain, ln1_bias, w_qkv, w_out, ln2_gain, ln2_bias, w_up, w_down
):
    half_rows, _, width = tokens.shape
    me = lax.axis_index("tensor")
    first = me == 0
    order = block_order(size, width)

    def assemble(array):
        ours = jnp.where(first, array[:, 0], array[:, 1])
        away = jnp.where(first, array[:, 1], array[:, 0])
        arrived = swap_tensor(away)
        rows = jnp.concatenate(
            [jnp.where(first, ours, arrived), jnp.where(first, arrived, ours)], axis=0
        )
        return mul(rows, order).astype(jnp.bfloat16)

    def disperse(rows):
        rows = mul(rows, order, NT).astype(jnp.bfloat16)
        ours = jnp.where(first, rows[:half_rows], rows[half_rows:])
        away = jnp.where(first, rows[half_rows:], rows[:half_rows])
        arrived = swap_tensor(away)
        return jnp.stack(
            [jnp.where(first, ours, arrived), jnp.where(first, arrived, ours)], axis=1
        )

    local_width = w_qkv.shape[2]
    pieces = local_width // 256
    step = local_width // pieces
    row_count = w_qkv.shape[1]
    qkv_shards = [
        w_qkv[:, :, p * step : (p + 1) * step].transpose(1, 0, 2).reshape(row_count, 3 * step)
        for p in range(pieces)
    ]
    params = jnp.stack([ln1_gain, ln1_bias, ln2_gain, ln2_bias])
    x16 = assemble(tokens)
    mask = size // 2
    while mask >= 1:
        params = jnp.concatenate([params, swap_dp(params, size, mask)], axis=1)
        mask //= 2
    gain_one, bias_one, gain_two, bias_two = (
        params[i : i + 1].astype(jnp.float32) for i in range(4)
    )
    qkv_w = [gather_pair(s, size, p % 2 == 0) for p, s in enumerate(qkv_shards)]
    out_w = gather_pair(w_out.T, size, True)
    hidden_step = w_up.shape[1] // 2
    up_w = [
        gather_pair(w_up[:, p * hidden_step : (p + 1) * hidden_step], size, p == 0)
        for p in range(2)
    ]
    down_t = w_down.T
    down_w = [
        gather_pair(down_t[:, p * hidden_step : (p + 1) * hidden_step], size, p == 0)
        for p in range(2)
    ]
    dy16 = assemble(d_out)

    x = x16.astype(jnp.float32)
    normed_one, normal_one, inverse_one = norm_rows(x, gain_one, bias_one)
    normed_one = normed_one.astype(jnp.bfloat16)
    attended = []
    for side in range(2):
        for p in range(pieces):
            qkv = mul(normed_one, qkv_w[p][side]).astype(jnp.bfloat16)
            attended.append((qkv,) + tuple(attend(qkv)))
    mixed = jnp.concatenate([a[1] for a in attended], axis=1)
    out_all = jnp.concatenate([out_w[0], out_w[1]], axis=1)
    hidden = x + mul(mixed, out_all, NT)
    normed_two, normal_two, inverse_two = norm_rows(hidden, gain_two, bias_two)
    normed_two = normed_two.astype(jnp.bfloat16)
    up_all = [up_w[p][side] for side in range(2) for p in range(2)]
    down_all = [down_w[p][side] for side in range(2) for p in range(2)]
    actives, slopes = [], []
    for w in up_all:
        active, slope = gelu_both(mul(normed_two, w))
        actives.append(active.astype(jnp.bfloat16))
        slopes.append(slope.astype(jnp.bfloat16))

    grad_down = [
        scatter_pair(dy16, actives[p], actives[2 + p], size, p == 0) for p in range(2)
    ]
    grad_upward = [
        (mul(dy16, w) * slope.astype(jnp.float32)).astype(jnp.bfloat16)
        for w, slope in zip(down_all, slopes)
    ]
    grad_up = [
        scatter_pair(normed_two, grad_upward[p], grad_upward[2 + p], size, p == 0)
        for p in range(2)
    ]
    down_cat = jnp.concatenate(down_all, axis=1)
    up_cat = jnp.concatenate(up_all, axis=1)
    block_out = (hidden + mul(jnp.concatenate(actives, axis=1), down_cat, NT)).astype(jnp.bfloat16)
    grad_normed_two = mul(jnp.concatenate(grad_upward, axis=1), up_cat, NT)
    grad_norm, gain_two_grad, bias_two_grad = norm_rows_grad(
        grad_normed_two, normal_two, inverse_two, gain_two
    )
    grad_hidden = dy16.astype(jnp.float32) + grad_norm
    low_hidden = grad_hidden.astype(jnp.bfloat16)

    grad_out = scatter_pair(
        low_hidden, mixed[:, :local_width], mixed[:, local_width:], size, True
    )
    grad_mixed = mul(low_hidden, out_all).astype(jnp.bfloat16)
    grad_qkv16 = []
    for n, (qkv, mixed_n, lse) in enumerate(attended):
        grad_qkv16.append(
            attend_grad(qkv, grad_mixed[:, n * step : (n + 1) * step], mixed_n, lse)
        )
    grad_qkv = [
        scatter_pair(normed_one, grad_qkv16[p], grad_qkv16[pieces + p], size, p % 2 == 0)
        for p in range(pieces)
    ]
    qkv_cat = jnp.concatenate([qkv_w[p][side] for side in range(2) for p in range(pieces)], axis=1)
    grad_normed_one = mul(jnp.concatenate(grad_qkv16, axis=1), qkv_cat, NT)
    grad_norm, gain_one_grad, bias_one_grad = norm_rows_grad(
        grad_normed_one, normal_one, inverse_one, gain_one
    )
    input_grad = (grad_hidden + grad_norm).astype(jnp.bfloat16)

    sums = jnp.concatenate([gain_one_grad, bias_one_grad, gain_two_grad, bias_two_grad], axis=0)
    mask = 1
    while mask < size:
        middle = sums.shape[1] // 2
        sums = sums[:, :middle] + swap_dp(sums[:, middle:], size, mask)
        mask *= 2
    sums = sums + swap_tensor(sums)

    return (
        disperse(block_out),
        disperse(input_grad),
        sums[0],
        sums[1],
        jnp.concatenate(
            [g.reshape(row_count, 3, step).transpose(1, 0, 2) for g in grad_qkv], axis=2
        ),
        grad_out.T,
        sums[2],
        sums[3],
        jnp.concatenate(grad_up, axis=1),
        jnp.concatenate(grad_down, axis=1).T,
    )


def solution(mesh):
    sizes = dict(mesh.shape)
    dp_size, tensor_size = sizes["dp"], sizes["tensor"]
    if tensor_size == 2 and dp_size >= 4 and dp_size & (dp_size - 1) == 0:
        body = functools.partial(on_device_whole, dp_size)
    else:
        body = on_device_shared
    placed = (
        P("tensor", "dp", None),
        P("tensor", "dp", None),
        P("dp"),
        P("dp"),
        P(None, "dp", "tensor"),
        P("tensor", "dp"),
        P("dp"),
        P("dp"),
        P("dp", "tensor"),
        P("tensor", "dp"),
    )
    return jax.shard_map(
        body,
        mesh=mesh,
        in_specs=placed,
        out_specs=(
            P("tensor", "dp", None),
            P("tensor", "dp", None),
            P("dp"),
            P("dp"),
            P(None, "dp", "tensor"),
            P("tensor", "dp"),
            P("dp"),
            P("dp"),
            P("dp", "tensor"),
            P("tensor", "dp"),
        ),
        check_vma=False,
    )
```

```python
import functools
import math

import jax
import jax.numpy as jnp
from jax import lax
from jax.experimental import pallas as pl
from jax.experimental.pallas import tpu as pltpu
from jax.sharding import PartitionSpec as P

HEAD_DIM = 64


EPSILON = 1e-05


def norm_rows(values, norm_gain, norm_bias):
    center = jnp.mean(values, axis=-1, keepdims=True)
    centered = values - center
    inverse = lax.rsqrt(jnp.mean(centered * centered, axis=-1, keepdims=True) + EPSILON)
    normal = centered * inverse
    return (normal * norm_gain + norm_bias, normal, inverse)


def norm_back(grad_in, normal, inverse, norm_gain):
    gain_grad = jnp.sum(grad_in * normal, axis=(0, 1))
    bias_grad = jnp.sum(grad_in, axis=(0, 1))
    scaled = grad_in * norm_gain
    first = jnp.mean(scaled, axis=-1, keepdims=True)
    second = jnp.mean(scaled * normal, axis=-1, keepdims=True)
    return (inverse * (scaled - first - normal * second), gain_grad, bias_grad)


def causal_mask(length):
    row_index = lax.broadcasted_iota(jnp.int32, (length, length), 0)
    column_index = lax.broadcasted_iota(jnp.int32, (length, length), 1)
    return column_index <= row_index


def attend_forward(triple):
    queries, key_rows, value_rows = triple
    scores = jnp.einsum(
        "qhd,khd->hqk", queries, key_rows, preferred_element_type=jnp.float32
    ) * HEAD_DIM ** (-0.5)
    scores = jnp.where(causal_mask(queries.shape[0]), scores, -1e30)
    row_max = jnp.max(scores, axis=-1, keepdims=True)
    weights = jnp.exp(scores - row_max)
    totals = jnp.sum(weights, axis=-1, keepdims=True)
    shares = (weights / totals).astype(jnp.bfloat16)
    mixed = jnp.einsum("hqk,khd->qhd", shares, value_rows, preferred_element_type=jnp.float32)
    return (mixed.astype(jnp.bfloat16), row_max + jnp.log(totals))


def attend_back(group):
    queries, key_rows, value_rows, grad_mixed, log_total = group
    factor = HEAD_DIM ** (-0.5)
    scores = (
        jnp.einsum("qhd,khd->hqk", queries, key_rows, preferred_element_type=jnp.float32) * factor
    )
    scores = jnp.where(causal_mask(queries.shape[0]), scores, -1e30)
    shares = jnp.exp(scores - log_total)
    grad_value = jnp.einsum(
        "hqk,qhd->khd", shares.astype(jnp.bfloat16), grad_mixed, preferred_element_type=jnp.float32
    )
    grad_shares = jnp.einsum(
        "qhd,khd->hqk", grad_mixed, value_rows, preferred_element_type=jnp.float32
    )
    inner = jnp.sum(shares * grad_shares, axis=-1, keepdims=True)
    grad_scores = (shares * (grad_shares - inner)).astype(jnp.bfloat16)
    grad_query = (
        jnp.einsum("hqk,khd->qhd", grad_scores, key_rows, preferred_element_type=jnp.float32)
        * factor
    )
    grad_key = (
        jnp.einsum("hqk,qhd->khd", grad_scores, queries, preferred_element_type=jnp.float32)
        * factor
    )
    return jnp.stack([grad_query, grad_key, grad_value]).astype(jnp.bfloat16)


def on_device_shared(tokens, d_out, ln1_gain, ln1_bias, w_qkv, w_out, ln2_gain, ln2_bias, w_up, w_down):
    local_rows, seq_count, width = tokens.shape
    gathered = (
        lax.all_gather(ln1_gain, "dp", axis=0, tiled=True),
        lax.all_gather(ln1_bias, "dp", axis=0, tiled=True),
        lax.all_gather(w_qkv, "dp", axis=1, tiled=True),
        lax.all_gather(w_out, "dp", axis=1, tiled=True),
        lax.all_gather(ln2_gain, "dp", axis=0, tiled=True),
        lax.all_gather(ln2_bias, "dp", axis=0, tiled=True),
        lax.all_gather(w_up, "dp", axis=0, tiled=True),
        lax.all_gather(w_down, "dp", axis=1, tiled=True),
    )
    gain_one, bias_one, qkv_weight, out_weight, gain_two, bias_two, up_weight, down_weight = (
        gathered
    )
    residual = tokens.astype(jnp.float32)
    normed_one, normal_one, inverse_one = norm_rows(
        residual, gain_one.astype(jnp.float32), bias_one.astype(jnp.float32)
    )
    low_one = normed_one.astype(jnp.bfloat16)
    rows_one = lax.all_gather(low_one, "tensor", axis=0, tiled=True)
    full_rows = rows_one.shape[0]
    projected = jnp.einsum(
        "tgd,cde->cgte", rows_one, qkv_weight, preferred_element_type=jnp.float32
    ).astype(jnp.bfloat16)
    local_width = projected.shape[3]
    heads_local = local_width // HEAD_DIM
    split_heads = projected.reshape(3, seq_count, full_rows, heads_local, HEAD_DIM)
    mixed, log_total = lax.map(attend_forward, (split_heads[0], split_heads[1], split_heads[2]))
    mixed = mixed.reshape(seq_count, full_rows, local_width)
    piece_rows = mixed
    hidden = residual + lax.psum_scatter(
        jnp.einsum(
            "gte,ed->tgd", piece_rows, out_weight, preferred_element_type=jnp.float32
        ).astype(jnp.bfloat16),
        "tensor",
        scatter_dimension=0,
        tiled=True,
    ).astype(jnp.float32)
    normed_two, normal_two, inverse_two = norm_rows(
        hidden, gain_two.astype(jnp.float32), bias_two.astype(jnp.float32)
    )
    low_two = normed_two.astype(jnp.bfloat16)
    rows_two = lax.all_gather(low_two, "tensor", axis=0, tiled=True)
    upward = jnp.einsum("tgd,df->tgf", rows_two, up_weight, preferred_element_type=jnp.float32)
    active = jax.nn.gelu(upward, approximate=True).astype(jnp.bfloat16)
    piece_rows = active
    block_sum = lax.psum_scatter(
        jnp.einsum(
            "tgf,fd->tgd", piece_rows, down_weight, preferred_element_type=jnp.float32
        ).astype(jnp.bfloat16),
        "tensor",
        scatter_dimension=0,
        tiled=True,
    ).astype(jnp.float32)
    block_out = (hidden + block_sum).astype(jnp.bfloat16)
    grad_rows = lax.all_gather(d_out, "tensor", axis=0, tiled=True)
    grad_down = jnp.einsum("tgf,tgd->fd", active, grad_rows, preferred_element_type=jnp.float32)
    grad_active = jnp.einsum(
        "tgd,fd->tgf", grad_rows, down_weight, preferred_element_type=jnp.float32
    )
    gelu_pull = jax.vjp(lambda inner: jax.nn.gelu(inner, approximate=True), upward)[1]
    grad_upward = gelu_pull(grad_active)[0].astype(jnp.bfloat16)
    grad_up = jnp.einsum("tgd,tgf->df", rows_two, grad_upward, preferred_element_type=jnp.float32)
    piece_rows = grad_upward
    grad_normed_two = lax.psum_scatter(
        jnp.einsum("tgf,df->tgd", piece_rows, up_weight, preferred_element_type=jnp.float32).astype(
            jnp.bfloat16
        ),
        "tensor",
        scatter_dimension=0,
        tiled=True,
    ).astype(jnp.float32)
    grad_hidden_norm, gain_two_grad, bias_two_grad = norm_back(
        grad_normed_two, normal_two, inverse_two, gain_two.astype(jnp.float32)
    )
    grad_hidden = d_out.astype(jnp.float32) + grad_hidden_norm
    low_hidden = grad_hidden.astype(jnp.bfloat16)
    hidden_rows = lax.all_gather(low_hidden, "tensor", axis=0, tiled=True)
    grad_out = jnp.einsum("gte,tgd->ed", mixed, hidden_rows, preferred_element_type=jnp.float32)
    grad_mixed = jnp.einsum(
        "tgd,ed->gte", hidden_rows, out_weight, preferred_element_type=jnp.float32
    ).astype(jnp.bfloat16)
    grad_heads = lax.map(
        attend_back,
        (
            split_heads[0],
            split_heads[1],
            split_heads[2],
            grad_mixed.reshape(seq_count, full_rows, heads_local, HEAD_DIM),
            log_total,
        ),
    )
    grad_projected = grad_heads.reshape(seq_count, 3, full_rows, local_width)
    grad_qkv = jnp.einsum(
        "tgd,gcte->cde", rows_one, grad_projected, preferred_element_type=jnp.float32
    )
    piece_rows = grad_projected
    grad_normed_one = lax.psum_scatter(
        jnp.einsum(
            "gcte,cde->tgd", piece_rows, qkv_weight, preferred_element_type=jnp.float32
        ).astype(jnp.bfloat16),
        "tensor",
        scatter_dimension=0,
        tiled=True,
    ).astype(jnp.float32)
    grad_input_norm, gain_one_grad, bias_one_grad = norm_back(
        grad_normed_one, normal_one, inverse_one, gain_one.astype(jnp.float32)
    )
    input_grad = (grad_hidden + grad_input_norm).astype(jnp.bfloat16)
    owned = (
        lax.psum_scatter(
            gain_one_grad.astype(jnp.bfloat16), "dp", scatter_dimension=0, tiled=True
        ).astype(jnp.float32),
        lax.psum_scatter(
            bias_one_grad.astype(jnp.bfloat16), "dp", scatter_dimension=0, tiled=True
        ).astype(jnp.float32),
        lax.psum_scatter(
            grad_qkv.astype(jnp.bfloat16), "dp", scatter_dimension=1, tiled=True
        ).astype(jnp.float32),
        lax.psum_scatter(
            grad_out.astype(jnp.bfloat16), "dp", scatter_dimension=1, tiled=True
        ).astype(jnp.float32),
        lax.psum_scatter(
            gain_two_grad.astype(jnp.bfloat16), "dp", scatter_dimension=0, tiled=True
        ).astype(jnp.float32),
        lax.psum_scatter(
            bias_two_grad.astype(jnp.bfloat16), "dp", scatter_dimension=0, tiled=True
        ).astype(jnp.float32),
        lax.psum_scatter(
            grad_up.astype(jnp.bfloat16), "dp", scatter_dimension=0, tiled=True
        ).astype(jnp.float32),
        lax.psum_scatter(
            grad_down.astype(jnp.bfloat16), "dp", scatter_dimension=1, tiled=True
        ).astype(jnp.float32),
    )
    norm_sums = lax.psum((owned[0], owned[1], owned[4], owned[5]), "tensor")
    return (
        block_out,
        input_grad,
        norm_sums[0],
        norm_sums[1],
        owned[2],
        owned[3],
        norm_sums[2],
        norm_sums[3],
        owned[6],
        owned[7],
    )


LOG2E = 1.4426950408889634
BLOCK = 256
NT = (((1,), (1,)), ((), ()))
TN = (((0,), (0,)), ((), ()))
NN = (((1,), (0,)), ((), ()))


def mul(left, right, dims=NN):
    return lax.dot_general(left, right, dims, preferred_element_type=jnp.float32)


def fwd_kernel(q_ref, k_ref, v_ref, o_ref, lse_ref):
    length = q_ref.shape[0]
    scale = LOG2E * HEAD_DIM**-0.5
    block = min(BLOCK, length)
    keep = lax.broadcasted_iota(jnp.int32, (block, block), 1) <= lax.broadcasted_iota(
        jnp.int32, (block, block), 0
    )
    heads = q_ref.shape[1] // HEAD_DIM
    for i in range(length // block):
        rows = slice(i * block, (i + 1) * block)
        outs = []
        for h in range(heads):
            cols = slice(h * HEAD_DIM, (h + 1) * HEAD_DIM)
            q = q_ref[rows, cols]
            diag = jnp.where(keep, mul(q, k_ref[rows, cols], NT), -1e30)
            top = jnp.max(diag, axis=1, keepdims=True)
            if i > 0:
                past = mul(q, k_ref[: i * block, cols], NT)
                top = jnp.maximum(top, jnp.max(past, axis=1, keepdims=True))
            shift = top * scale
            w = jnp.exp2(diag * scale - shift)
            total = jnp.sum(w, axis=1, keepdims=True)
            out = mul(w.astype(jnp.bfloat16), v_ref[rows, cols])
            if i > 0:
                w = jnp.exp2(past * scale - shift)
                total = total + jnp.sum(w, axis=1, keepdims=True)
                out = out + mul(w.astype(jnp.bfloat16), v_ref[: i * block, cols])
            outs.append(out / total)
            lse = shift + jnp.log2(total)
            lse_ref[0, h : h + 1, rows] = jnp.broadcast_to(lse, (block, 128)).T[:1]
        o_ref[rows, :] = jnp.concatenate(outs, axis=1).astype(jnp.bfloat16)


def attend(qkv):
    length, width3 = qkv.shape
    width = width3 // 3
    pairs = width // 128
    return pl.pallas_call(
        fwd_kernel,
        grid=(pairs,),
        in_specs=[
            pl.BlockSpec((length, 128), lambda j: (0, j)),
            pl.BlockSpec((length, 128), lambda j: (0, pairs + j)),
            pl.BlockSpec((length, 128), lambda j: (0, 2 * pairs + j)),
        ],
        out_specs=[
            pl.BlockSpec((length, 128), lambda j: (0, j)),
            pl.BlockSpec((1, 8, length), lambda j: (j, 0, 0)),
        ],
        out_shape=[
            jax.ShapeDtypeStruct((length, width), jnp.bfloat16),
            jax.ShapeDtypeStruct((pairs, 8, length), jnp.float32),
        ],
        compiler_params=pltpu.CompilerParams(vmem_limit_bytes=40 * 2**20),
        cost_estimate=pl.CostEstimate(
            flops=8 * length * length * width, bytes_accessed=8 * length * width, transcendentals=0
        ),
    )(qkv, qkv, qkv)


def back_kernel(q_ref, k_ref, v_ref, do_ref, o_ref, lse_ref, dqkv_ref):
    length = q_ref.shape[0]
    width = dqkv_ref.shape[1] // 3
    factor = HEAD_DIM**-0.5
    scale = LOG2E * factor
    block = min(BLOCK, length)
    keep = lax.broadcasted_iota(jnp.int32, (block, block), 0) <= lax.broadcasted_iota(
        jnp.int32, (block, block), 1
    )
    count = length // block
    heads = q_ref.shape[1] // HEAD_DIM
    col = pl.program_id(0) * 128
    both = do_ref[...].astype(jnp.float32) * o_ref[...].astype(jnp.float32)
    both = both.T
    deltas = [
        jnp.sum(both[h * HEAD_DIM : (h + 1) * HEAD_DIM], axis=0, keepdims=True)
        for h in range(heads)
    ]
    dqs = [[None] * count for _ in range(heads)]
    for j in range(count):
        rows = slice(j * block, (j + 1) * block)
        dks, dvs = [], []
        for h in range(heads):
            cols = slice(h * HEAD_DIM, (h + 1) * HEAD_DIM)
            k, v = k_ref[rows, cols], v_ref[rows, cols]
            q, do = q_ref[j * block :, cols], do_ref[j * block :, cols]
            lse = lse_ref[0, h : h + 1, j * block :]
            w = jnp.exp2(mul(k, q, NT) * scale - lse)
            if j + 1 < count:
                w = jnp.concatenate([jnp.where(keep, w[:, :block], 0.0), w[:, block:]], axis=1)
            else:
                w = jnp.where(keep, w, 0.0)
            ds = (w * (mul(v, do, NT) - deltas[h][:, j * block :])).astype(jnp.bfloat16)
            dvs.append(mul(w.astype(jnp.bfloat16), do))
            dks.append(mul(ds, q) * factor)
            dq = mul(ds, k, TN)
            for i in range(j, count):
                part = dq[(i - j) * block : (i - j + 1) * block]
                dqs[h][i] = part if dqs[h][i] is None else dqs[h][i] + part
        dqkv_ref[rows, pl.ds(pl.multiple_of(width + col, 128), 128)] = jnp.concatenate(
            dks, axis=1
        ).astype(jnp.bfloat16)
        dqkv_ref[rows, pl.ds(pl.multiple_of(2 * width + col, 128), 128)] = jnp.concatenate(
            dvs, axis=1
        ).astype(jnp.bfloat16)
        dqkv_ref[rows, pl.ds(pl.multiple_of(col, 128), 128)] = (
            jnp.concatenate([dqs[h][j] for h in range(heads)], axis=1) * factor
        ).astype(jnp.bfloat16)


def attend_grad(qkv, grad_mixed, mixed, lse):
    length, width3 = qkv.shape
    width = width3 // 3
    pairs = width // 128
    return pl.pallas_call(
        back_kernel,
        grid=(pairs,),
        in_specs=[
            pl.BlockSpec((length, 128), lambda j: (0, j)),
            pl.BlockSpec((length, 128), lambda j: (0, pairs + j)),
            pl.BlockSpec((length, 128), lambda j: (0, 2 * pairs + j)),
            pl.BlockSpec((length, 128), lambda j: (0, j)),
            pl.BlockSpec((length, 128), lambda j: (0, j)),
            pl.BlockSpec((1, 8, length), lambda j: (j, 0, 0)),
        ],
        out_specs=pl.BlockSpec((length, width3), lambda j: (0, 0)),
        out_shape=jax.ShapeDtypeStruct((length, width3), jnp.bfloat16),
        compiler_params=pltpu.CompilerParams(vmem_limit_bytes=40 * 2**20),
        cost_estimate=pl.CostEstimate(
            flops=20 * length * length * width, bytes_accessed=16 * length * width, transcendentals=0
        ),
    )(qkv, qkv, qkv, grad_mixed, mixed, lse)


def swap_dp(array, size, mask):
    return lax.ppermute(array, "dp", [(i, i ^ mask) for i in range(size)])


def swap_tensor(array):
    return lax.ppermute(array, "tensor", [(0, 1), (1, 0)])


def add_low(left, right):
    return (left.astype(jnp.float32) + right.astype(jnp.float32)).astype(jnp.bfloat16)


def sum_kernel(count, *refs):
    total = mul(refs[0][...], refs[count][...], NT)
    for i in range(1, count):
        total = total + mul(refs[i][...], refs[count + i][...], NT)
    refs[2 * count][...] = total


def sum_products(lefts, rights):
    rows, columns = lefts[0].shape[0], rights[0].shape[0]
    block = min(256, rows)
    depth = sum(left.shape[1] for left in lefts)
    return pl.pallas_call(
        functools.partial(sum_kernel, len(lefts)),
        grid=(rows // block,),
        in_specs=[pl.BlockSpec((block, left.shape[1]), lambda i: (i, 0)) for left in lefts]
        + [pl.BlockSpec(right.shape, lambda i: (0, 0)) for right in rights],
        out_specs=pl.BlockSpec((block, columns), lambda i: (i, 0)),
        out_shape=jax.ShapeDtypeStruct((rows, columns), jnp.float32),
        compiler_params=pltpu.CompilerParams(vmem_limit_bytes=40 * 2**20),
        cost_estimate=pl.CostEstimate(
            flops=2 * rows * columns * depth,
            bytes_accessed=2 * (rows + columns) * depth + 4 * rows * columns,
            transcendentals=0,
        ),
    )(*lefts, *rights)


def stack_rows(array, arrived):
    return jnp.concatenate([array, arrived], axis=0)


def low_half(array):
    return array[: array.shape[0] // 2]


def high_half(array):
    return array[array.shape[0] // 2 :]


def away_rows(rows, columns):
    half = rows.shape[1] // 2
    return mul(rows[:, half:], columns, TN).astype(jnp.bfloat16)


def kept_rows(rows, columns, arrived):
    half = rows.shape[1] // 2
    return (mul(rows[:, :half], columns, TN) + arrived.astype(jnp.float32)).astype(jnp.bfloat16)


def fold_dp(array, size, mask):
    return add_low(low_half(array), swap_dp(high_half(array), size, mask))


class Steps:
    def __init__(self):
        self.live = {}

    def __getattr__(self, name):
        return self.live[name]

    def put(self, **arrays):
        self.live.update(arrays)

    def drop(self, *names):
        for name in names:
            del self.live[name]

    def cut(self):
        names = list(self.live)
        arrays = lax.optimization_barrier(tuple(self.live[name] for name in names))
        self.live = dict(zip(names, arrays))


def norm_rows_grad(grad_in, normal, inverse, norm_gain):
    gain_grad = jnp.sum(grad_in * normal, axis=0, keepdims=True)
    bias_grad = jnp.sum(grad_in, axis=0, keepdims=True)
    scaled = grad_in * norm_gain
    first = jnp.mean(scaled, axis=-1, keepdims=True)
    second = jnp.mean(scaled * normal, axis=-1, keepdims=True)
    return (inverse * (scaled - first - normal * second), gain_grad, bias_grad)


def block_order(size, width):
    block = width // size
    here = lax.axis_index("dp")
    column = lax.broadcasted_iota(jnp.int32, (width, width), 1)
    place, inside = column // block, column % block
    source = here
    bit, value = size // 2, 1
    while bit >= 1:
        source = source ^ jnp.where((place // bit) % 2 == 1, value, 0)
        bit //= 2
        value *= 2
    row = lax.broadcasted_iota(jnp.int32, (width, width), 0)
    return (row == source * block + inside).astype(jnp.bfloat16)


def gelu_both(u):
    inner = math.sqrt(2 / math.pi)
    t = jnp.tanh(inner * (u + 0.044715 * u * u * u))
    slope = 0.5 * (1.0 + t) + 0.5 * u * (1.0 - t * t) * inner * (1.0 + 3 * 0.044715 * u * u)
    return 0.5 * u * (1.0 + t), slope


def on_device_whole(
    size, tokens, d_out, ln1_gain, ln1_bias, w_qkv, w_out, ln2_gain, ln2_bias, w_up, w_down
):
    half_rows, _, width = tokens.shape
    first = lax.axis_index("tensor") == 0
    far, near = size // 2, size // 4

    def split(array):
        return (
            jnp.where(first, array[:, 0], array[:, 1]),
            jnp.where(first, array[:, 1], array[:, 0]),
        )

    def join(ours, arrived, order):
        rows = jnp.concatenate(
            [jnp.where(first, ours, arrived), jnp.where(first, arrived, ours)], axis=0
        )
        return mul(rows, order).astype(jnp.bfloat16)

    def reorder(rows, order):
        return mul(rows, order, NT).astype(jnp.bfloat16)

    def part(rows):
        low, high = rows[:half_rows], rows[half_rows:]
        return jnp.where(first, low, high), jnp.where(first, high, low)

    def place(ours, arrived):
        return jnp.stack(
            [jnp.where(first, ours, arrived), jnp.where(first, arrived, ours)], axis=1
        )

    def grow(array, mask):
        return stack_rows(array, swap_dp(array, size, mask))

    def grow_params(array, mask):
        return jnp.concatenate([array, swap_dp(array, size, mask)], axis=1)

    row_count, local_width = w_qkv.shape[1:]
    step = local_width // 2
    qkv_a, qkv_b = (
        w_qkv[:, :, p * step : (p + 1) * step].transpose(1, 0, 2).reshape(row_count, 3 * step)
        for p in range(2)
    )
    s = Steps()

    ours, away = split(tokens)
    arriving = swap_tensor(away)
    s.put(a=grow(qkv_a, far), b=grow(qkv_b, far))
    s.put(par=grow_params(jnp.stack([ln1_gain, ln1_bias, ln2_gain, ln2_bias]), far))
    s.put(o=w_out.T, u=w_up, d=w_down.T, ours=ours, order=block_order(size, width), d_out=d_out)
    s.cut()
    s.put(a=grow(s.a, near), b=grow(s.b, near), o=grow(s.o, far), par=grow_params(s.par, near))
    s.put(arrived=arriving)
    s.cut()
    s.put(ax=swap_tensor(s.a), a=grow(s.a, 2), o=grow(s.o, near), par=grow_params(s.par, 2))
    arriving = grow(s.u, far)
    s.put(x16=join(s.ours, s.arrived, s.order))
    s.drop("ours", "arrived")
    s.cut()
    s.put(a_own=grow(s.a, 1), b=grow(s.b, 2), ox=swap_tensor(s.o), par=grow_params(s.par, 1))
    s.put(u=arriving)
    gain_one, bias_one, gain_two, bias_two = (
        s.par[i : i + 1].astype(jnp.float32) for i in range(4)
    )
    normed, normal, inverse = norm_rows(s.x16.astype(jnp.float32), gain_one, bias_one)
    s.put(n1=normed.astype(jnp.bfloat16), normal1=normal, inverse1=inverse)
    s.put(gain_one=gain_one, gain_two=gain_two, bias_two=bias_two)
    s.drop("a", "par")
    s.cut()
    b_arriving = swap_tensor(s.b)
    arriving = grow(s.u, near)
    s.put(b_own=grow(s.b, 1), ax=grow(s.ax, 2))
    qkv = mul(s.n1, s.a_own).astype(jnp.bfloat16)
    mixed, lse = attend(qkv)
    s.put(qkv0=qkv, mixed0=mixed, lse0=lse)
    s.drop("b")
    s.cut()
    s.put(a_oth=grow(s.ax, 1), o=grow(s.o, 2), ox=grow(s.ox, 2))
    qkv = mul(s.n1, s.b_own).astype(jnp.bfloat16)
    mixed, lse = attend(qkv)
    s.put(qkv1=qkv, mixed1=mixed, lse1=lse, bx=b_arriving, u=arriving)
    s.drop("ax")
    s.cut()
    x_arriving = swap_tensor(s.u)
    y_arriving = grow(s.u, 2)
    s.put(b_oth=grow(s.bx, 1), o=grow(s.o, 1), ox=grow(s.ox, 1), d=grow(s.d, far))
    qkv = mul(s.n1, s.a_oth).astype(jnp.bfloat16)
    mixed, lse = attend(qkv)
    s.put(qkv2=qkv, mixed2=mixed, lse2=lse)
    s.drop("bx")
    s.cut()
    s.put(d=grow(s.d, near))
    qkv = mul(s.n1, s.b_oth).astype(jnp.bfloat16)
    mixed, lse = attend(qkv)
    s.put(qkv3=qkv, mixed3=mixed, lse3=lse, ux=x_arriving, u=y_arriving)
    s.cut()
    y_arriving = grow(s.ux, 2)
    ours, away = split(s.d_out)
    x_arriving = swap_tensor(away)
    s.put(u_own=grow(s.u, 1))
    mixed = jnp.concatenate([s.mixed0, s.mixed1, s.mixed2, s.mixed3], axis=1)
    out_all = jnp.concatenate([s.o, s.ox], axis=1)
    hidden = s.x16.astype(jnp.float32) + mul(mixed, out_all, NT)
    normed, normal, inverse = norm_rows(hidden, s.gain_two, s.bias_two)
    s.put(mixed=mixed, out_all=out_all, hidden=hidden, n2=normed.astype(jnp.bfloat16))
    s.put(normal2=normal, inverse2=inverse, ours=ours)
    s.drop("u", "o", "ox", "x16", "d_out", "bias_two")
    s.cut()
    active, slope = gelu_both(mul(s.n2, s.u_own))
    s.put(active0=active.astype(jnp.bfloat16), slope0=slope.astype(jnp.bfloat16))
    s.put(ux=y_arriving, arrived=x_arriving)
    s.cut()
    s.put(u_oth=grow(s.ux, 1))
    x_arriving = swap_tensor(s.d)
    y_arriving = grow(s.d, 2)
    dy16 = join(s.ours, s.arrived, s.order)
    away0 = away_rows(dy16, s.active0)
    s.put(dy16=dy16, down0=swap_dp(away0, size, 1))
    s.drop("ux", "ours", "arrived")
    s.cut()
    active, slope = gelu_both(mul(s.n2, s.u_oth))
    s.put(active1=active.astype(jnp.bfloat16), slope1=slope.astype(jnp.bfloat16))
    s.put(dx=x_arriving, d=y_arriving)
    s.cut()
    y_arriving = grow(s.dx, 2)
    s.put(d_own=grow(s.d, 1))
    away1 = away_rows(s.dy16, s.active1)
    s.put(down1=swap_dp(away1, size, 1), down0=kept_rows(s.dy16, s.active0, s.down0))
    s.drop("d")
    s.cut()
    grad = mul(s.dy16, s.d_own) * s.slope0.astype(jnp.float32)
    s.put(up_grad0=grad.astype(jnp.bfloat16), down1=kept_rows(s.dy16, s.active1, s.down1))
    s.put(dx=y_arriving)
    s.drop("slope0")
    s.cut()
    down_arriving = swap_tensor(s.down1)
    s.put(d_oth=grow(s.dx, 1))
    s.put(up0=swap_dp(away_rows(s.n2, s.up_grad0), size, 1))
    s.drop("dx", "down1")
    s.cut()
    grad = mul(s.dy16, s.d_oth) * s.slope1.astype(jnp.float32)
    grad = grad.astype(jnp.bfloat16)
    s.put(up_grad1=grad, up1=swap_dp(away_rows(s.n2, grad), size, 1))
    s.put(up0=kept_rows(s.n2, s.up_grad0, s.up0))
    s.drop("slope1")
    s.cut()
    total = sum_products([s.active0, s.active1], [s.d_own, s.d_oth])
    rows = reorder((s.hidden + total).astype(jnp.bfloat16), s.order)
    ours, away = part(rows)
    s.put(ours=ours, away=away, up1=kept_rows(s.n2, s.up_grad1, s.up1))
    s.drop("active0", "active1", "d_own", "d_oth", "hidden", "n2")
    s.cut()
    s.put(down0=add_low(s.down0, down_arriving))
    s.cut()
    x_arriving = swap_tensor(s.away)
    s.put(down0=fold_dp(s.down0, size, 2))
    s.put(grad_n2=sum_products([s.up_grad0, s.up_grad1], [s.u_own, s.u_oth]))
    s.drop("away", "up_grad0", "up_grad1", "u_own", "u_oth")
    s.cut()
    up0_arriving = fold_dp(s.up0, size, 2)
    up1_arriving = fold_dp(s.up1, size, 2)
    s.put(down0=fold_dp(s.down0, size, near))
    grad_norm, gain_two_grad, bias_two_grad = norm_rows_grad(
        s.grad_n2, s.normal2, s.inverse2, s.gain_two
    )
    grad_hidden = s.dy16.astype(jnp.float32) + grad_norm
    low_hidden = grad_hidden.astype(jnp.bfloat16)
    s.put(gain_two_grad=gain_two_grad, bias_two_grad=bias_two_grad, grad_hidden=grad_hidden)
    s.put(low_hidden=low_hidden, grad_mixed=mul(low_hidden, s.out_all).astype(jnp.bfloat16))
    s.put(out0=swap_dp(away_rows(low_hidden, s.mixed[:, :local_width]), size, 1))
    s.put(out1=swap_dp(away_rows(low_hidden, s.mixed[:, local_width:]), size, 1))
    s.drop("grad_n2", "normal2", "inverse2", "gain_two", "out_all", "dy16", "up0", "up1")
    s.cut()
    down_grad = swap_dp(high_half(s.down0), size, far).astype(jnp.float32)
    s.put(down=low_half(s.down0).astype(jnp.float32) + down_grad)
    s.put(out0=kept_rows(s.low_hidden, s.mixed[:, :local_width], s.out0))
    s.put(out1=kept_rows(s.low_hidden, s.mixed[:, local_width:], s.out1))
    s.put(dqkv0=attend_grad(s.qkv0, s.grad_mixed[:, :step], s.mixed0, s.lse0))
    s.drop("low_hidden", "mixed", "qkv0", "mixed0", "lse0", "down0")
    s.cut()
    s.put(out0=add_low(s.out0, swap_tensor(s.out1)), block_away=x_arriving)
    s.put(dqkv2=attend_grad(s.qkv2, s.grad_mixed[:, 2 * step : 3 * step], s.mixed2, s.lse2))
    s.drop("out1", "qkv2", "mixed2", "lse2")
    s.cut()
    s.put(a0=swap_dp(away_rows(s.n1, s.dqkv0), size, 1))
    s.put(a1=swap_dp(away_rows(s.n1, s.dqkv2), size, 1))
    s.put(dqkv1=attend_grad(s.qkv1, s.grad_mixed[:, step : 2 * step], s.mixed1, s.lse1))
    s.put(up0=up0_arriving, up1=up1_arriving)
    s.drop("qkv1", "mixed1", "lse1")
    s.cut()
    arriving = swap_tensor(s.up1)
    s.put(out0=fold_dp(s.out0, size, 2))
    s.put(a0=kept_rows(s.n1, s.dqkv0, s.a0), a1=kept_rows(s.n1, s.dqkv2, s.a1))
    s.put(dqkv3=attend_grad(s.qkv3, s.grad_mixed[:, 3 * step :], s.mixed3, s.lse3))
    s.drop("up1", "qkv3", "mixed3", "lse3", "grad_mixed")
    s.cut()
    a0, a1 = fold_dp(s.a0, size, 2), fold_dp(s.a1, size, 2)
    s.put(b0=swap_dp(away_rows(s.n1, s.dqkv1), size, 1))
    s.put(b1=swap_dp(away_rows(s.n1, s.dqkv3), size, 1))
    s.put(out0=fold_dp(s.out0, size, near))
    s.put(
        grad_n1=sum_products(
            [s.dqkv0, s.dqkv1, s.dqkv2, s.dqkv3], [s.a_own, s.b_own, s.a_oth, s.b_oth]
        )
    )
    s.put(up0=add_low(s.up0, arriving), a0=a0, a1=a1)
    s.drop("dqkv0", "dqkv2", "a_own", "b_own", "a_oth", "b_oth")
    s.cut()
    s.put(up0=fold_dp(s.up0, size, near))
    s.put(b0=kept_rows(s.n1, s.dqkv1, s.b0), b1=kept_rows(s.n1, s.dqkv3, s.b1))
    grad_norm, gain_one_grad, bias_one_grad = norm_rows_grad(
        s.grad_n1, s.normal1, s.inverse1, s.gain_one
    )
    rows = reorder((s.grad_hidden + grad_norm).astype(jnp.bfloat16), s.order)
    ours, away = part(rows)
    s.put(input_ours=ours, input_away=away)
    s.put(
        sums=jnp.concatenate(
            [gain_one_grad, bias_one_grad, s.gain_two_grad, s.bias_two_grad], axis=0
        )
    )
    s.cut()
    input_grad = place(s.input_ours, swap_tensor(s.input_away))
    block_out = place(s.ours, s.block_away)

    def last_folds(array):
        array = fold_dp(array, size, near)
        arrived = swap_dp(high_half(array), size, far)
        return low_half(array).astype(jnp.float32) + arrived.astype(jnp.float32)

    def last_fold(array):
        arrived = swap_dp(high_half(array), size, far)
        return low_half(array).astype(jnp.float32) + arrived.astype(jnp.float32)

    grad_a = last_folds(add_low(s.a0, swap_tensor(s.a1)))
    b0, b1 = fold_dp(s.b0, size, 2), fold_dp(s.b1, size, 2)
    grad_b = last_folds(add_low(b0, swap_tensor(b1)))
    grad_up = last_fold(s.up0)
    grad_out = last_fold(s.out0)
    sums = s.sums
    mask = 1
    while mask < size:
        middle = sums.shape[1] // 2
        sums = sums[:, :middle] + swap_dp(sums[:, middle:], size, mask)
        mask *= 2
    sums = sums + swap_tensor(sums)

    return (
        block_out,
        input_grad,
        sums[0],
        sums[1],
        jnp.concatenate(
            [g.reshape(row_count, 3, step).transpose(1, 0, 2) for g in (grad_a, grad_b)], axis=2
        ),
        grad_out.T,
        sums[2],
        sums[3],
        grad_up,
        s.down.T,
    )


def solution(mesh):
    sizes = dict(mesh.shape)
    dp_size, tensor_size = sizes["dp"], sizes["tensor"]
    if tensor_size == 2 and dp_size == 16:
        body = functools.partial(on_device_whole, dp_size)
    else:
        body = on_device_shared
    placed = (
        P("tensor", "dp", None),
        P("tensor", "dp", None),
        P("dp"),
        P("dp"),
        P(None, "dp", "tensor"),
        P("tensor", "dp"),
        P("dp"),
        P("dp"),
        P("dp", "tensor"),
        P("tensor", "dp"),
    )
    return jax.shard_map(
        body,
        mesh=mesh,
        in_specs=placed,
        out_specs=(
            P("tensor", "dp", None),
            P("tensor", "dp", None),
            P("dp"),
            P("dp"),
            P(None, "dp", "tensor"),
            P("tensor", "dp"),
            P("dp"),
            P("dp"),
            P("dp", "tensor"),
            P("tensor", "dp"),
        ),
        check_vma=False,
    )
```

```python
import functools
import math

import jax
import jax.numpy as jnp
from jax import lax
from jax.experimental import pallas as pl
from jax.experimental.pallas import tpu as pltpu
from jax.sharding import PartitionSpec as P

HEAD_DIM = 64


EPSILON = 1e-05


def norm_rows(values, norm_gain, norm_bias):
    center = jnp.mean(values, axis=-1, keepdims=True)
    centered = values - center
    inverse = lax.rsqrt(jnp.mean(centered * centered, axis=-1, keepdims=True) + EPSILON)
    normal = centered * inverse
    return (normal * norm_gain + norm_bias, normal, inverse)


def norm_back(grad_in, normal, inverse, norm_gain):
    gain_grad = jnp.sum(grad_in * normal, axis=(0, 1))
    bias_grad = jnp.sum(grad_in, axis=(0, 1))
    scaled = grad_in * norm_gain
    first = jnp.mean(scaled, axis=-1, keepdims=True)
    second = jnp.mean(scaled * normal, axis=-1, keepdims=True)
    return (inverse * (scaled - first - normal * second), gain_grad, bias_grad)


def causal_mask(length):
    row_index = lax.broadcasted_iota(jnp.int32, (length, length), 0)
    column_index = lax.broadcasted_iota(jnp.int32, (length, length), 1)
    return column_index <= row_index


def attend_forward(triple):
    queries, key_rows, value_rows = triple
    scores = jnp.einsum(
        "qhd,khd->hqk", queries, key_rows, preferred_element_type=jnp.float32
    ) * HEAD_DIM ** (-0.5)
    scores = jnp.where(causal_mask(queries.shape[0]), scores, -1e30)
    row_max = jnp.max(scores, axis=-1, keepdims=True)
    weights = jnp.exp(scores - row_max)
    totals = jnp.sum(weights, axis=-1, keepdims=True)
    shares = (weights / totals).astype(jnp.bfloat16)
    mixed = jnp.einsum("hqk,khd->qhd", shares, value_rows, preferred_element_type=jnp.float32)
    return (mixed.astype(jnp.bfloat16), row_max + jnp.log(totals))


def attend_back(group):
    queries, key_rows, value_rows, grad_mixed, log_total = group
    factor = HEAD_DIM ** (-0.5)
    scores = (
        jnp.einsum("qhd,khd->hqk", queries, key_rows, preferred_element_type=jnp.float32) * factor
    )
    scores = jnp.where(causal_mask(queries.shape[0]), scores, -1e30)
    shares = jnp.exp(scores - log_total)
    grad_value = jnp.einsum(
        "hqk,qhd->khd", shares.astype(jnp.bfloat16), grad_mixed, preferred_element_type=jnp.float32
    )
    grad_shares = jnp.einsum(
        "qhd,khd->hqk", grad_mixed, value_rows, preferred_element_type=jnp.float32
    )
    inner = jnp.sum(shares * grad_shares, axis=-1, keepdims=True)
    grad_scores = (shares * (grad_shares - inner)).astype(jnp.bfloat16)
    grad_query = (
        jnp.einsum("hqk,khd->qhd", grad_scores, key_rows, preferred_element_type=jnp.float32)
        * factor
    )
    grad_key = (
        jnp.einsum("hqk,qhd->khd", grad_scores, queries, preferred_element_type=jnp.float32)
        * factor
    )
    return jnp.stack([grad_query, grad_key, grad_value]).astype(jnp.bfloat16)


def on_device_shared(tokens, d_out, ln1_gain, ln1_bias, w_qkv, w_out, ln2_gain, ln2_bias, w_up, w_down):
    local_rows, seq_count, width = tokens.shape
    gathered = (
        lax.all_gather(ln1_gain, "dp", axis=0, tiled=True),
        lax.all_gather(ln1_bias, "dp", axis=0, tiled=True),
        lax.all_gather(w_qkv, "dp", axis=1, tiled=True),
        lax.all_gather(w_out, "dp", axis=1, tiled=True),
        lax.all_gather(ln2_gain, "dp", axis=0, tiled=True),
        lax.all_gather(ln2_bias, "dp", axis=0, tiled=True),
        lax.all_gather(w_up, "dp", axis=0, tiled=True),
        lax.all_gather(w_down, "dp", axis=1, tiled=True),
    )
    gain_one, bias_one, qkv_weight, out_weight, gain_two, bias_two, up_weight, down_weight = (
        gathered
    )
    residual = tokens.astype(jnp.float32)
    normed_one, normal_one, inverse_one = norm_rows(
        residual, gain_one.astype(jnp.float32), bias_one.astype(jnp.float32)
    )
    low_one = normed_one.astype(jnp.bfloat16)
    rows_one = lax.all_gather(low_one, "tensor", axis=0, tiled=True)
    full_rows = rows_one.shape[0]
    projected = jnp.einsum(
        "tgd,cde->cgte", rows_one, qkv_weight, preferred_element_type=jnp.float32
    ).astype(jnp.bfloat16)
    local_width = projected.shape[3]
    heads_local = local_width // HEAD_DIM
    split_heads = projected.reshape(3, seq_count, full_rows, heads_local, HEAD_DIM)
    mixed, log_total = lax.map(attend_forward, (split_heads[0], split_heads[1], split_heads[2]))
    mixed = mixed.reshape(seq_count, full_rows, local_width)
    piece_rows = mixed
    hidden = residual + lax.psum_scatter(
        jnp.einsum(
            "gte,ed->tgd", piece_rows, out_weight, preferred_element_type=jnp.float32
        ).astype(jnp.bfloat16),
        "tensor",
        scatter_dimension=0,
        tiled=True,
    ).astype(jnp.float32)
    normed_two, normal_two, inverse_two = norm_rows(
        hidden, gain_two.astype(jnp.float32), bias_two.astype(jnp.float32)
    )
    low_two = normed_two.astype(jnp.bfloat16)
    rows_two = lax.all_gather(low_two, "tensor", axis=0, tiled=True)
    upward = jnp.einsum("tgd,df->tgf", rows_two, up_weight, preferred_element_type=jnp.float32)
    active = jax.nn.gelu(upward, approximate=True).astype(jnp.bfloat16)
    piece_rows = active
    block_sum = lax.psum_scatter(
        jnp.einsum(
            "tgf,fd->tgd", piece_rows, down_weight, preferred_element_type=jnp.float32
        ).astype(jnp.bfloat16),
        "tensor",
        scatter_dimension=0,
        tiled=True,
    ).astype(jnp.float32)
    block_out = (hidden + block_sum).astype(jnp.bfloat16)
    grad_rows = lax.all_gather(d_out, "tensor", axis=0, tiled=True)
    grad_down = jnp.einsum("tgf,tgd->fd", active, grad_rows, preferred_element_type=jnp.float32)
    grad_active = jnp.einsum(
        "tgd,fd->tgf", grad_rows, down_weight, preferred_element_type=jnp.float32
    )
    gelu_pull = jax.vjp(lambda inner: jax.nn.gelu(inner, approximate=True), upward)[1]
    grad_upward = gelu_pull(grad_active)[0].astype(jnp.bfloat16)
    grad_up = jnp.einsum("tgd,tgf->df", rows_two, grad_upward, preferred_element_type=jnp.float32)
    piece_rows = grad_upward
    grad_normed_two = lax.psum_scatter(
        jnp.einsum("tgf,df->tgd", piece_rows, up_weight, preferred_element_type=jnp.float32).astype(
            jnp.bfloat16
        ),
        "tensor",
        scatter_dimension=0,
        tiled=True,
    ).astype(jnp.float32)
    grad_hidden_norm, gain_two_grad, bias_two_grad = norm_back(
        grad_normed_two, normal_two, inverse_two, gain_two.astype(jnp.float32)
    )
    grad_hidden = d_out.astype(jnp.float32) + grad_hidden_norm
    low_hidden = grad_hidden.astype(jnp.bfloat16)
    hidden_rows = lax.all_gather(low_hidden, "tensor", axis=0, tiled=True)
    grad_out = jnp.einsum("gte,tgd->ed", mixed, hidden_rows, preferred_element_type=jnp.float32)
    grad_mixed = jnp.einsum(
        "tgd,ed->gte", hidden_rows, out_weight, preferred_element_type=jnp.float32
    ).astype(jnp.bfloat16)
    grad_heads = lax.map(
        attend_back,
        (
            split_heads[0],
            split_heads[1],
            split_heads[2],
            grad_mixed.reshape(seq_count, full_rows, heads_local, HEAD_DIM),
            log_total,
        ),
    )
    grad_projected = grad_heads.reshape(seq_count, 3, full_rows, local_width)
    grad_qkv = jnp.einsum(
        "tgd,gcte->cde", rows_one, grad_projected, preferred_element_type=jnp.float32
    )
    piece_rows = grad_projected
    grad_normed_one = lax.psum_scatter(
        jnp.einsum(
            "gcte,cde->tgd", piece_rows, qkv_weight, preferred_element_type=jnp.float32
        ).astype(jnp.bfloat16),
        "tensor",
        scatter_dimension=0,
        tiled=True,
    ).astype(jnp.float32)
    grad_input_norm, gain_one_grad, bias_one_grad = norm_back(
        grad_normed_one, normal_one, inverse_one, gain_one.astype(jnp.float32)
    )
    input_grad = (grad_hidden + grad_input_norm).astype(jnp.bfloat16)
    owned = (
        lax.psum_scatter(
            gain_one_grad.astype(jnp.bfloat16), "dp", scatter_dimension=0, tiled=True
        ).astype(jnp.float32),
        lax.psum_scatter(
            bias_one_grad.astype(jnp.bfloat16), "dp", scatter_dimension=0, tiled=True
        ).astype(jnp.float32),
        lax.psum_scatter(
            grad_qkv.astype(jnp.bfloat16), "dp", scatter_dimension=1, tiled=True
        ).astype(jnp.float32),
        lax.psum_scatter(
            grad_out.astype(jnp.bfloat16), "dp", scatter_dimension=1, tiled=True
        ).astype(jnp.float32),
        lax.psum_scatter(
            gain_two_grad.astype(jnp.bfloat16), "dp", scatter_dimension=0, tiled=True
        ).astype(jnp.float32),
        lax.psum_scatter(
            bias_two_grad.astype(jnp.bfloat16), "dp", scatter_dimension=0, tiled=True
        ).astype(jnp.float32),
        lax.psum_scatter(
            grad_up.astype(jnp.bfloat16), "dp", scatter_dimension=0, tiled=True
        ).astype(jnp.float32),
        lax.psum_scatter(
            grad_down.astype(jnp.bfloat16), "dp", scatter_dimension=1, tiled=True
        ).astype(jnp.float32),
    )
    norm_sums = lax.psum((owned[0], owned[1], owned[4], owned[5]), "tensor")
    return (
        block_out,
        input_grad,
        norm_sums[0],
        norm_sums[1],
        owned[2],
        owned[3],
        norm_sums[2],
        norm_sums[3],
        owned[6],
        owned[7],
    )


LOG2E = 1.4426950408889634
BLOCK = 256
NT = (((1,), (1,)), ((), ()))
TN = (((0,), (0,)), ((), ()))
NN = (((1,), (0,)), ((), ()))


def mul(left, right, dims=NN):
    return lax.dot_general(left, right, dims, preferred_element_type=jnp.float32)


def fwd_kernel(q_ref, k_ref, v_ref, o_ref, lse_ref):
    length = q_ref.shape[0]
    scale = LOG2E * HEAD_DIM**-0.5
    block = min(BLOCK, length)
    keep = lax.broadcasted_iota(jnp.int32, (block, block), 1) <= lax.broadcasted_iota(
        jnp.int32, (block, block), 0
    )
    heads = q_ref.shape[1] // HEAD_DIM
    for i in range(length // block):
        rows = slice(i * block, (i + 1) * block)
        outs = []
        for h in range(heads):
            cols = slice(h * HEAD_DIM, (h + 1) * HEAD_DIM)
            q = q_ref[rows, cols]
            diag = jnp.where(keep, mul(q, k_ref[rows, cols], NT), -1e30)
            top = jnp.max(diag, axis=1, keepdims=True)
            if i > 0:
                past = mul(q, k_ref[: i * block, cols], NT)
                top = jnp.maximum(top, jnp.max(past, axis=1, keepdims=True))
            shift = top * scale
            w = jnp.exp2(diag * scale - shift)
            total = jnp.sum(w, axis=1, keepdims=True)
            out = mul(w.astype(jnp.bfloat16), v_ref[rows, cols])
            if i > 0:
                w = jnp.exp2(past * scale - shift)
                total = total + jnp.sum(w, axis=1, keepdims=True)
                out = out + mul(w.astype(jnp.bfloat16), v_ref[: i * block, cols])
            outs.append(out / total)
            lse = shift + jnp.log2(total)
            lse_ref[0, h : h + 1, rows] = jnp.broadcast_to(lse, (block, 128)).T[:1]
        o_ref[rows, :] = jnp.concatenate(outs, axis=1).astype(jnp.bfloat16)


def attend(qkv):
    length, width3 = qkv.shape
    width = width3 // 3
    pairs = width // 128
    return pl.pallas_call(
        fwd_kernel,
        grid=(pairs,),
        in_specs=[
            pl.BlockSpec((length, 128), lambda j: (0, j)),
            pl.BlockSpec((length, 128), lambda j: (0, pairs + j)),
            pl.BlockSpec((length, 128), lambda j: (0, 2 * pairs + j)),
        ],
        out_specs=[
            pl.BlockSpec((length, 128), lambda j: (0, j)),
            pl.BlockSpec((1, 8, length), lambda j: (j, 0, 0)),
        ],
        out_shape=[
            jax.ShapeDtypeStruct((length, width), jnp.bfloat16),
            jax.ShapeDtypeStruct((pairs, 8, length), jnp.float32),
        ],
        compiler_params=pltpu.CompilerParams(vmem_limit_bytes=40 * 2**20),
        cost_estimate=pl.CostEstimate(
            flops=8 * length * length * width, bytes_accessed=8 * length * width, transcendentals=0
        ),
    )(qkv, qkv, qkv)


def back_kernel(q_ref, k_ref, v_ref, do_ref, o_ref, lse_ref, dqkv_ref):
    length = q_ref.shape[0]
    width = dqkv_ref.shape[1] // 3
    factor = HEAD_DIM**-0.5
    scale = LOG2E * factor
    block = min(BLOCK, length)
    keep = lax.broadcasted_iota(jnp.int32, (block, block), 0) <= lax.broadcasted_iota(
        jnp.int32, (block, block), 1
    )
    count = length // block
    heads = q_ref.shape[1] // HEAD_DIM
    col = pl.program_id(0) * 128
    both = do_ref[...].astype(jnp.float32) * o_ref[...].astype(jnp.float32)
    both = both.T
    deltas = [
        jnp.sum(both[h * HEAD_DIM : (h + 1) * HEAD_DIM], axis=0, keepdims=True)
        for h in range(heads)
    ]
    dqs = [[None] * count for _ in range(heads)]
    for j in range(count):
        rows = slice(j * block, (j + 1) * block)
        dks, dvs = [], []
        for h in range(heads):
            cols = slice(h * HEAD_DIM, (h + 1) * HEAD_DIM)
            k, v = k_ref[rows, cols], v_ref[rows, cols]
            q, do = q_ref[j * block :, cols], do_ref[j * block :, cols]
            lse = lse_ref[0, h : h + 1, j * block :]
            w = jnp.exp2(mul(k, q, NT) * scale - lse)
            if j + 1 < count:
                w = jnp.concatenate([jnp.where(keep, w[:, :block], 0.0), w[:, block:]], axis=1)
            else:
                w = jnp.where(keep, w, 0.0)
            ds = (w * (mul(v, do, NT) - deltas[h][:, j * block :])).astype(jnp.bfloat16)
            dvs.append(mul(w.astype(jnp.bfloat16), do))
            dks.append(mul(ds, q) * factor)
            dq = mul(ds, k, TN)
            for i in range(j, count):
                part = dq[(i - j) * block : (i - j + 1) * block]
                dqs[h][i] = part if dqs[h][i] is None else dqs[h][i] + part
        dqkv_ref[rows, pl.ds(pl.multiple_of(width + col, 128), 128)] = jnp.concatenate(
            dks, axis=1
        ).astype(jnp.bfloat16)
        dqkv_ref[rows, pl.ds(pl.multiple_of(2 * width + col, 128), 128)] = jnp.concatenate(
            dvs, axis=1
        ).astype(jnp.bfloat16)
        dqkv_ref[rows, pl.ds(pl.multiple_of(col, 128), 128)] = (
            jnp.concatenate([dqs[h][j] for h in range(heads)], axis=1) * factor
        ).astype(jnp.bfloat16)


def attend_grad(qkv, grad_mixed, mixed, lse):
    length, width3 = qkv.shape
    width = width3 // 3
    pairs = width // 128
    return pl.pallas_call(
        back_kernel,
        grid=(pairs,),
        in_specs=[
            pl.BlockSpec((length, 128), lambda j: (0, j)),
            pl.BlockSpec((length, 128), lambda j: (0, pairs + j)),
            pl.BlockSpec((length, 128), lambda j: (0, 2 * pairs + j)),
            pl.BlockSpec((length, 128), lambda j: (0, j)),
            pl.BlockSpec((length, 128), lambda j: (0, j)),
            pl.BlockSpec((1, 8, length), lambda j: (j, 0, 0)),
        ],
        out_specs=pl.BlockSpec((length, width3), lambda j: (0, 0)),
        out_shape=jax.ShapeDtypeStruct((length, width3), jnp.bfloat16),
        compiler_params=pltpu.CompilerParams(vmem_limit_bytes=40 * 2**20),
        cost_estimate=pl.CostEstimate(
            flops=20 * length * length * width, bytes_accessed=16 * length * width, transcendentals=0
        ),
    )(qkv, qkv, qkv, grad_mixed, mixed, lse)


def swap_dp(array, size, mask):
    return lax.ppermute(array, "dp", [(i, i ^ mask) for i in range(size)])


def swap_tensor(array):
    return lax.ppermute(array, "tensor", [(0, 1), (1, 0)])


def add_low(left, right):
    return (left.astype(jnp.float32) + right.astype(jnp.float32)).astype(jnp.bfloat16)


def sum_kernel(count, *refs):
    total = mul(refs[0][...], refs[count][...], NT)
    for i in range(1, count):
        total = total + mul(refs[i][...], refs[count + i][...], NT)
    refs[2 * count][...] = total


def sum_products(lefts, rights):
    rows, columns = lefts[0].shape[0], rights[0].shape[0]
    block = min(256, rows)
    depth = sum(left.shape[1] for left in lefts)
    return pl.pallas_call(
        functools.partial(sum_kernel, len(lefts)),
        grid=(rows // block,),
        in_specs=[pl.BlockSpec((block, left.shape[1]), lambda i: (i, 0)) for left in lefts]
        + [pl.BlockSpec(right.shape, lambda i: (0, 0)) for right in rights],
        out_specs=pl.BlockSpec((block, columns), lambda i: (i, 0)),
        out_shape=jax.ShapeDtypeStruct((rows, columns), jnp.float32),
        compiler_params=pltpu.CompilerParams(vmem_limit_bytes=40 * 2**20),
        cost_estimate=pl.CostEstimate(
            flops=2 * rows * columns * depth,
            bytes_accessed=2 * (rows + columns) * depth + 4 * rows * columns,
            transcendentals=0,
        ),
    )(*lefts, *rights)


def stack_rows(array, arrived):
    return jnp.concatenate([array, arrived], axis=0)


def low_half(array):
    return array[: array.shape[0] // 2]


def high_half(array):
    return array[array.shape[0] // 2 :]


def away_rows(rows, columns):
    half = rows.shape[1] // 2
    return mul(rows[:, half:], columns, TN).astype(jnp.bfloat16)


def kept_rows(rows, columns, arrived):
    half = rows.shape[1] // 2
    return (mul(rows[:, :half], columns, TN) + arrived.astype(jnp.float32)).astype(jnp.bfloat16)


def fold_dp(array, size, mask):
    return add_low(low_half(array), swap_dp(high_half(array), size, mask))


class Steps:
    def __init__(self):
        self.live = {}

    def __getattr__(self, name):
        return self.live[name]

    def put(self, **arrays):
        self.live.update(arrays)

    def drop(self, *names):
        for name in names:
            del self.live[name]

    def cut(self):
        names = list(self.live)
        arrays = lax.optimization_barrier(tuple(self.live[name] for name in names))
        self.live = dict(zip(names, arrays))


def norm_rows_grad(grad_in, normal, inverse, norm_gain):
    gain_grad = jnp.sum(grad_in * normal, axis=0, keepdims=True)
    bias_grad = jnp.sum(grad_in, axis=0, keepdims=True)
    scaled = grad_in * norm_gain
    first = jnp.mean(scaled, axis=-1, keepdims=True)
    second = jnp.mean(scaled * normal, axis=-1, keepdims=True)
    return (inverse * (scaled - first - normal * second), gain_grad, bias_grad)


def block_order(size, width):
    block = width // size
    here = lax.axis_index("dp")
    column = lax.broadcasted_iota(jnp.int32, (width, width), 1)
    place, inside = column // block, column % block
    source = here
    bit, value = size // 2, 1
    while bit >= 1:
        source = source ^ jnp.where((place // bit) % 2 == 1, value, 0)
        bit //= 2
        value *= 2
    row = lax.broadcasted_iota(jnp.int32, (width, width), 0)
    return (row == source * block + inside).astype(jnp.bfloat16)


def gelu_both(u):
    first = math.sqrt(2 / math.pi)
    third = 0.044715 * first
    square = u * u
    h = 0.5 * jnp.tanh(u * (first + third * square)) + 0.5
    slope = h + (h - h * h) * (u * (2 * first + 6 * third * square))
    return u * h, slope


def on_device_whole(
    size, tokens, d_out, ln1_gain, ln1_bias, w_qkv, w_out, ln2_gain, ln2_bias, w_up, w_down
):
    half_rows, _, width = tokens.shape
    first = lax.axis_index("tensor") == 0
    far, near = size // 2, size // 4

    def split(array):
        me = lax.axis_index("tensor")
        return (
            lax.dynamic_index_in_dim(array, me, 1, keepdims=False),
            lax.dynamic_index_in_dim(array, 1 - me, 1, keepdims=False),
        )

    def join(ours, arrived, order):
        rows = jnp.concatenate(
            [jnp.where(first, ours, arrived), jnp.where(first, arrived, ours)], axis=0
        )
        return mul(rows, order).astype(jnp.bfloat16)

    def reorder(rows, order):
        return mul(rows, order, NT).astype(jnp.bfloat16)

    def part(rows):
        low, high = rows[:half_rows], rows[half_rows:]
        return jnp.where(first, low, high), jnp.where(first, high, low)

    def place(ours, arrived):
        return jnp.stack(
            [jnp.where(first, ours, arrived), jnp.where(first, arrived, ours)], axis=1
        )

    def grow(array, mask):
        return stack_rows(array, swap_dp(array, size, mask))

    def grow_params(array, mask):
        return jnp.concatenate([array, swap_dp(array, size, mask)], axis=1)

    row_count, local_width = w_qkv.shape[1:]
    step = local_width // 2
    qkv_a, qkv_b = (
        w_qkv[:, :, p * step : (p + 1) * step].transpose(1, 0, 2).reshape(row_count, 3 * step)
        for p in range(2)
    )
    s = Steps()

    ours, away = split(tokens)
    tokens_arriving = swap_tensor(away)
    s.put(a=grow(qkv_a, far), b=grow(qkv_b, far))
    s.put(par=grow_params(jnp.stack([ln1_gain, ln1_bias, ln2_gain, ln2_bias]), far))
    s.put(o=w_out.T, u=w_up, d=w_down.T, ours=ours, order=block_order(size, width), d_out=d_out)
    s.cut()
    u_arriving = grow(s.u, far)
    s.put(a=grow(s.a, near), b=grow(s.b, near), o=grow(s.o, far), par=grow_params(s.par, near))
    s.put(arrived=tokens_arriving)
    s.cut()
    s.put(ax=swap_tensor(s.a), a=grow(s.a, 2), o=grow(s.o, near), par=grow_params(s.par, 2))
    s.put(x16=join(s.ours, s.arrived, s.order), u=u_arriving)
    s.drop("ours", "arrived")
    s.cut()
    u_arriving = grow(s.u, near)
    d_arriving = grow(s.d, far)
    s.put(a_own=grow(s.a, 1), b=grow(s.b, 2), ox=swap_tensor(s.o), par=grow_params(s.par, 1))
    gain_one, bias_one, gain_two, bias_two = (
        s.par[i : i + 1].astype(jnp.float32) for i in range(4)
    )
    normed, normal, inverse = norm_rows(s.x16.astype(jnp.float32), gain_one, bias_one)
    s.put(n1=normed.astype(jnp.bfloat16), normal1=normal, inverse1=inverse)
    s.put(gain_one=gain_one, gain_two=gain_two, bias_two=bias_two)
    s.drop("a", "par")
    s.cut()
    b_arriving = swap_tensor(s.b)
    s.put(b_own=grow(s.b, 1), ax=grow(s.ax, 2))
    qkv = mul(s.n1, s.a_own).astype(jnp.bfloat16)
    mixed, lse = attend(qkv)
    s.put(qkv0=qkv, mixed0=mixed, lse0=lse, u=u_arriving)
    s.drop("b")
    s.cut()
    ux_arriving = swap_tensor(s.u)
    s.put(a_oth=grow(s.ax, 1), o=grow(s.o, 2), ox=grow(s.ox, 2))
    u_arriving = grow(s.u, 2)
    qkv = mul(s.n1, s.b_own).astype(jnp.bfloat16)
    mixed, lse = attend(qkv)
    s.put(qkv1=qkv, mixed1=mixed, lse1=lse, bx=b_arriving, d=d_arriving)
    s.drop("ax")
    s.cut()
    d_arriving = grow(s.d, near)
    s.put(b_oth=grow(s.bx, 1), o=grow(s.o, 1), ox=grow(s.ox, 1))
    qkv = mul(s.n1, s.a_oth).astype(jnp.bfloat16)
    mixed, lse = attend(qkv)
    s.put(qkv2=qkv, mixed2=mixed, lse2=lse, ux=ux_arriving, u=u_arriving, d=d_arriving)
    s.drop("bx")
    s.cut()
    ux_arriving = grow(s.ux, 2)
    dx_arriving = swap_tensor(s.d)
    s.put(u_own=grow(s.u, 1))
    qkv = mul(s.n1, s.b_oth).astype(jnp.bfloat16)
    mixed, lse = attend(qkv)
    s.put(qkv3=qkv, mixed3=mixed, lse3=lse)
    s.drop("u")
    s.cut()
    mixed = jnp.concatenate([s.mixed0, s.mixed1, s.mixed2, s.mixed3], axis=1)
    out_all = jnp.concatenate([s.o, s.ox], axis=1)
    hidden = s.x16.astype(jnp.float32) + mul(mixed, out_all, NT)
    normed, normal, inverse = norm_rows(hidden, s.gain_two, s.bias_two)
    s.put(mixed=mixed, out_all=out_all, hidden=hidden, n2=normed.astype(jnp.bfloat16))
    s.put(normal2=normal, inverse2=inverse, ux=ux_arriving, dx=dx_arriving)
    s.drop("o", "ox", "x16", "bias_two")
    s.cut()
    ours, away = split(s.d_out)
    cot_arriving = swap_tensor(away)
    d_arriving = grow(s.d, 2)
    s.put(u_oth=grow(s.ux, 1), ours=ours)
    active, slope = gelu_both(mul(s.n2, s.u_own))
    s.put(active0=active.astype(jnp.bfloat16), slope0=slope.astype(jnp.bfloat16))
    s.drop("d_out", "ux")
    s.cut()
    active, slope = gelu_both(mul(s.n2, s.u_oth))
    s.put(active1=active.astype(jnp.bfloat16), slope1=slope.astype(jnp.bfloat16))
    s.put(arrived=cot_arriving, d=d_arriving)
    s.cut()
    dx_arriving = grow(s.dx, 2)
    s.put(d_own=grow(s.d, 1))
    dy16 = join(s.ours, s.arrived, s.order)
    s.put(dy16=dy16, down0=swap_dp(away_rows(dy16, s.active0), size, 1))
    s.put(down1=swap_dp(away_rows(dy16, s.active1), size, 1))
    s.drop("d", "ours", "arrived")
    s.cut()
    grad = mul(s.dy16, s.d_own) * s.slope0.astype(jnp.float32)
    s.put(up_grad0=grad.astype(jnp.bfloat16), dx=dx_arriving)
    s.put(down0=kept_rows(s.dy16, s.active0, s.down0), down1=kept_rows(s.dy16, s.active1, s.down1))
    s.drop("slope0")
    s.cut()
    down_arriving = swap_tensor(s.down1)
    d_oth = grow(s.dx, 1)
    up0 = swap_dp(away_rows(s.n2, s.up_grad0), size, 1)
    grad = (mul(s.dy16, d_oth) * s.slope1.astype(jnp.float32)).astype(jnp.bfloat16)
    s.put(d_oth=d_oth, up_grad1=grad, up1=swap_dp(away_rows(s.n2, grad), size, 1))
    s.put(up0=kept_rows(s.n2, s.up_grad0, up0))
    s.drop("dx", "down1", "slope1")
    s.cut()
    up0_arriving = fold_dp(s.up0, size, 2)
    total = sum_products([s.active0, s.active1], [s.d_own, s.d_oth])
    rows = reorder((s.hidden + total).astype(jnp.bfloat16), s.order)
    ours, away = part(rows)
    s.put(ours=ours, away=away, up1=kept_rows(s.n2, s.up_grad1, s.up1))
    s.drop("active0", "active1", "d_own", "d_oth", "hidden", "n2", "up0")
    s.cut()
    up1_arriving = fold_dp(s.up1, size, 2)
    s.put(grad_n2=sum_products([s.up_grad0, s.up_grad1], [s.u_own, s.u_oth]))
    s.put(down0=add_low(s.down0, down_arriving))
    s.drop("up_grad0", "up_grad1", "u_own", "u_oth", "up1")
    s.cut()
    block_arriving = swap_tensor(s.away)
    grad_norm, gain_two_grad, bias_two_grad = norm_rows_grad(
        s.grad_n2, s.normal2, s.inverse2, s.gain_two
    )
    grad_hidden = s.dy16.astype(jnp.float32) + grad_norm
    low_hidden = grad_hidden.astype(jnp.bfloat16)
    s.put(gain_two_grad=gain_two_grad, bias_two_grad=bias_two_grad, grad_hidden=grad_hidden)
    s.put(low_hidden=low_hidden, grad_mixed=mul(low_hidden, s.out_all).astype(jnp.bfloat16))
    s.put(out0=swap_dp(away_rows(low_hidden, s.mixed[:, :local_width]), size, 1))
    s.put(out1=swap_dp(away_rows(low_hidden, s.mixed[:, local_width:]), size, 1))
    s.drop("grad_n2", "normal2", "inverse2", "gain_two", "out_all", "dy16", "away")
    s.cut()
    s.put(out0=kept_rows(s.low_hidden, s.mixed[:, :local_width], s.out0))
    s.put(out1=kept_rows(s.low_hidden, s.mixed[:, local_width:], s.out1))
    s.put(dqkv0=attend_grad(s.qkv0, s.grad_mixed[:, :step], s.mixed0, s.lse0))
    s.put(up0=up0_arriving, up1=up1_arriving)
    s.drop("low_hidden", "mixed", "qkv0", "mixed0", "lse0")
    s.cut()
    down_arriving = fold_dp(s.down0, size, 2)
    out_arriving = swap_tensor(s.out1)
    s.put(dqkv2=attend_grad(s.qkv2, s.grad_mixed[:, 2 * step : 3 * step], s.mixed2, s.lse2))
    s.put(block_arrived=block_arriving)
    s.drop("out1", "qkv2", "mixed2", "lse2", "down0")
    s.cut()
    up_arriving = swap_tensor(s.up1)
    s.put(a0=swap_dp(away_rows(s.n1, s.dqkv0), size, 1))
    s.put(a1=swap_dp(away_rows(s.n1, s.dqkv2), size, 1))
    s.put(dqkv1=attend_grad(s.qkv1, s.grad_mixed[:, step : 2 * step], s.mixed1, s.lse1))
    s.put(down0=down_arriving, out0=add_low(s.out0, out_arriving))
    s.drop("qkv1", "mixed1", "lse1", "up1")
    s.cut()
    s.put(down0=fold_dp(s.down0, size, near), out0=fold_dp(s.out0, size, 2))
    s.put(a0=kept_rows(s.n1, s.dqkv0, s.a0), a1=kept_rows(s.n1, s.dqkv2, s.a1))
    s.put(dqkv3=attend_grad(s.qkv3, s.grad_mixed[:, 3 * step :], s.mixed3, s.lse3))
    s.put(up0=add_low(s.up0, up_arriving))
    s.drop("qkv3", "mixed3", "lse3", "grad_mixed")
    s.cut()

    def last_fold(array):
        arrived = swap_dp(high_half(array), size, far)
        return low_half(array).astype(jnp.float32) + arrived.astype(jnp.float32)

    a_arriving = swap_tensor(s.a1)
    s.put(b0=swap_dp(away_rows(s.n1, s.dqkv1), size, 1))
    s.put(b1=swap_dp(away_rows(s.n1, s.dqkv3), size, 1))
    s.put(up0=fold_dp(s.up0, size, near), out0=fold_dp(s.out0, size, near))
    s.put(grad_down=last_fold(s.down0))
    s.put(
        grad_n1=sum_products(
            [s.dqkv0, s.dqkv1, s.dqkv2, s.dqkv3], [s.a_own, s.b_own, s.a_oth, s.b_oth]
        )
    )
    s.drop("dqkv0", "dqkv2", "a_own", "b_own", "a_oth", "b_oth", "a1", "down0")
    s.cut()
    b1 = kept_rows(s.n1, s.dqkv3, s.b1)
    b_arriving = swap_tensor(b1)
    s.put(a0=add_low(s.a0, a_arriving))
    s.put(b0=kept_rows(s.n1, s.dqkv1, s.b0))
    s.put(grad_up=last_fold(s.up0), grad_out=last_fold(s.out0))
    grad_norm, gain_one_grad, bias_one_grad = norm_rows_grad(
        s.grad_n1, s.normal1, s.inverse1, s.gain_one
    )
    rows = reorder((s.grad_hidden + grad_norm).astype(jnp.bfloat16), s.order)
    ours, away = part(rows)
    s.put(input_ours=ours, input_away=away)
    s.put(
        sums=jnp.concatenate(
            [gain_one_grad, bias_one_grad, s.gain_two_grad, s.bias_two_grad], axis=0
        )
    )
    s.put(block_out=place(s.ours, s.block_arrived), grad_down=s.grad_down.T)
    s.drop("ours", "block_arrived", "b1", "up0", "out0", "dqkv1", "dqkv3", "n1", "grad_n1")
    s.cut()
    input_grad = place(s.input_ours, swap_tensor(s.input_away))
    grad_a = last_fold(fold_dp(fold_dp(s.a0, size, 2), size, near))
    grad_b = last_fold(fold_dp(fold_dp(add_low(s.b0, b_arriving), size, 2), size, near))
    sums = s.sums
    mask = 1
    while mask < size:
        middle = sums.shape[1] // 2
        sums = sums[:, :middle] + swap_dp(sums[:, middle:], size, mask)
        mask *= 2
    sums = sums + swap_tensor(sums)

    return (
        s.block_out,
        input_grad,
        sums[0],
        sums[1],
        jnp.concatenate(
            [g.reshape(row_count, 3, step).transpose(1, 0, 2) for g in (grad_a, grad_b)], axis=2
        ),
        s.grad_out.T,
        sums[2],
        sums[3],
        s.grad_up,
        s.grad_down,
    )


def solution(mesh):
    sizes = dict(mesh.shape)
    dp_size, tensor_size = sizes["dp"], sizes["tensor"]
    if tensor_size == 2 and dp_size == 16:
        body = functools.partial(on_device_whole, dp_size)
    else:
        body = on_device_shared
    placed = (
        P("tensor", "dp", None),
        P("tensor", "dp", None),
        P("dp"),
        P("dp"),
        P(None, "dp", "tensor"),
        P("tensor", "dp"),
        P("dp"),
        P("dp"),
        P("dp", "tensor"),
        P("tensor", "dp"),
    )
    return jax.shard_map(
        body,
        mesh=mesh,
        in_specs=placed,
        out_specs=(
            P("tensor", "dp", None),
            P("tensor", "dp", None),
            P("dp"),
            P("dp"),
            P(None, "dp", "tensor"),
            P("tensor", "dp"),
            P("dp"),
            P("dp"),
            P("dp", "tensor"),
            P("tensor", "dp"),
        ),
        check_vma=False,
    )
```

```python
import functools
import math

import jax
import jax.numpy as jnp
from jax import lax
from jax.experimental import pallas as pl
from jax.experimental.pallas import tpu as pltpu
from jax.sharding import PartitionSpec as P

HEAD_DIM = 64


EPSILON = 1e-05


def norm_rows(values, norm_gain, norm_bias):
    center = jnp.mean(values, axis=-1, keepdims=True)
    centered = values - center
    inverse = lax.rsqrt(jnp.mean(centered * centered, axis=-1, keepdims=True) + EPSILON)
    normal = centered * inverse
    return (normal * norm_gain + norm_bias, normal, inverse)


def norm_back(grad_in, normal, inverse, norm_gain):
    gain_grad = jnp.sum(grad_in * normal, axis=(0, 1))
    bias_grad = jnp.sum(grad_in, axis=(0, 1))
    scaled = grad_in * norm_gain
    first = jnp.mean(scaled, axis=-1, keepdims=True)
    second = jnp.mean(scaled * normal, axis=-1, keepdims=True)
    return (inverse * (scaled - first - normal * second), gain_grad, bias_grad)


def causal_mask(length):
    row_index = lax.broadcasted_iota(jnp.int32, (length, length), 0)
    column_index = lax.broadcasted_iota(jnp.int32, (length, length), 1)
    return column_index <= row_index


def attend_forward(triple):
    queries, key_rows, value_rows = triple
    scores = jnp.einsum(
        "qhd,khd->hqk", queries, key_rows, preferred_element_type=jnp.float32
    ) * HEAD_DIM ** (-0.5)
    scores = jnp.where(causal_mask(queries.shape[0]), scores, -1e30)
    row_max = jnp.max(scores, axis=-1, keepdims=True)
    weights = jnp.exp(scores - row_max)
    totals = jnp.sum(weights, axis=-1, keepdims=True)
    shares = (weights / totals).astype(jnp.bfloat16)
    mixed = jnp.einsum("hqk,khd->qhd", shares, value_rows, preferred_element_type=jnp.float32)
    return (mixed.astype(jnp.bfloat16), row_max + jnp.log(totals))


def attend_back(group):
    queries, key_rows, value_rows, grad_mixed, log_total = group
    factor = HEAD_DIM ** (-0.5)
    scores = (
        jnp.einsum("qhd,khd->hqk", queries, key_rows, preferred_element_type=jnp.float32) * factor
    )
    scores = jnp.where(causal_mask(queries.shape[0]), scores, -1e30)
    shares = jnp.exp(scores - log_total)
    grad_value = jnp.einsum(
        "hqk,qhd->khd", shares.astype(jnp.bfloat16), grad_mixed, preferred_element_type=jnp.float32
    )
    grad_shares = jnp.einsum(
        "qhd,khd->hqk", grad_mixed, value_rows, preferred_element_type=jnp.float32
    )
    inner = jnp.sum(shares * grad_shares, axis=-1, keepdims=True)
    grad_scores = (shares * (grad_shares - inner)).astype(jnp.bfloat16)
    grad_query = (
        jnp.einsum("hqk,khd->qhd", grad_scores, key_rows, preferred_element_type=jnp.float32)
        * factor
    )
    grad_key = (
        jnp.einsum("hqk,qhd->khd", grad_scores, queries, preferred_element_type=jnp.float32)
        * factor
    )
    return jnp.stack([grad_query, grad_key, grad_value]).astype(jnp.bfloat16)


def on_device_shared(tokens, d_out, ln1_gain, ln1_bias, w_qkv, w_out, ln2_gain, ln2_bias, w_up, w_down):
    local_rows, seq_count, width = tokens.shape
    gathered = (
        lax.all_gather(ln1_gain, "dp", axis=0, tiled=True),
        lax.all_gather(ln1_bias, "dp", axis=0, tiled=True),
        lax.all_gather(w_qkv, "dp", axis=1, tiled=True),
        lax.all_gather(w_out, "dp", axis=1, tiled=True),
        lax.all_gather(ln2_gain, "dp", axis=0, tiled=True),
        lax.all_gather(ln2_bias, "dp", axis=0, tiled=True),
        lax.all_gather(w_up, "dp", axis=0, tiled=True),
        lax.all_gather(w_down, "dp", axis=1, tiled=True),
    )
    gain_one, bias_one, qkv_weight, out_weight, gain_two, bias_two, up_weight, down_weight = (
        gathered
    )
    residual = tokens.astype(jnp.float32)
    normed_one, normal_one, inverse_one = norm_rows(
        residual, gain_one.astype(jnp.float32), bias_one.astype(jnp.float32)
    )
    low_one = normed_one.astype(jnp.bfloat16)
    rows_one = lax.all_gather(low_one, "tensor", axis=0, tiled=True)
    full_rows = rows_one.shape[0]
    projected = jnp.einsum(
        "tgd,cde->cgte", rows_one, qkv_weight, preferred_element_type=jnp.float32
    ).astype(jnp.bfloat16)
    local_width = projected.shape[3]
    heads_local = local_width // HEAD_DIM
    split_heads = projected.reshape(3, seq_count, full_rows, heads_local, HEAD_DIM)
    mixed, log_total = lax.map(attend_forward, (split_heads[0], split_heads[1], split_heads[2]))
    mixed = mixed.reshape(seq_count, full_rows, local_width)
    piece_rows = mixed
    hidden = residual + lax.psum_scatter(
        jnp.einsum(
            "gte,ed->tgd", piece_rows, out_weight, preferred_element_type=jnp.float32
        ).astype(jnp.bfloat16),
        "tensor",
        scatter_dimension=0,
        tiled=True,
    ).astype(jnp.float32)
    normed_two, normal_two, inverse_two = norm_rows(
        hidden, gain_two.astype(jnp.float32), bias_two.astype(jnp.float32)
    )
    low_two = normed_two.astype(jnp.bfloat16)
    rows_two = lax.all_gather(low_two, "tensor", axis=0, tiled=True)
    upward = jnp.einsum("tgd,df->tgf", rows_two, up_weight, preferred_element_type=jnp.float32)
    active = jax.nn.gelu(upward, approximate=True).astype(jnp.bfloat16)
    piece_rows = active
    block_sum = lax.psum_scatter(
        jnp.einsum(
            "tgf,fd->tgd", piece_rows, down_weight, preferred_element_type=jnp.float32
        ).astype(jnp.bfloat16),
        "tensor",
        scatter_dimension=0,
        tiled=True,
    ).astype(jnp.float32)
    block_out = (hidden + block_sum).astype(jnp.bfloat16)
    grad_rows = lax.all_gather(d_out, "tensor", axis=0, tiled=True)
    grad_down = jnp.einsum("tgf,tgd->fd", active, grad_rows, preferred_element_type=jnp.float32)
    grad_active = jnp.einsum(
        "tgd,fd->tgf", grad_rows, down_weight, preferred_element_type=jnp.float32
    )
    gelu_pull = jax.vjp(lambda inner: jax.nn.gelu(inner, approximate=True), upward)[1]
    grad_upward = gelu_pull(grad_active)[0].astype(jnp.bfloat16)
    grad_up = jnp.einsum("tgd,tgf->df", rows_two, grad_upward, preferred_element_type=jnp.float32)
    piece_rows = grad_upward
    grad_normed_two = lax.psum_scatter(
        jnp.einsum("tgf,df->tgd", piece_rows, up_weight, preferred_element_type=jnp.float32).astype(
            jnp.bfloat16
        ),
        "tensor",
        scatter_dimension=0,
        tiled=True,
    ).astype(jnp.float32)
    grad_hidden_norm, gain_two_grad, bias_two_grad = norm_back(
        grad_normed_two, normal_two, inverse_two, gain_two.astype(jnp.float32)
    )
    grad_hidden = d_out.astype(jnp.float32) + grad_hidden_norm
    low_hidden = grad_hidden.astype(jnp.bfloat16)
    hidden_rows = lax.all_gather(low_hidden, "tensor", axis=0, tiled=True)
    grad_out = jnp.einsum("gte,tgd->ed", mixed, hidden_rows, preferred_element_type=jnp.float32)
    grad_mixed = jnp.einsum(
        "tgd,ed->gte", hidden_rows, out_weight, preferred_element_type=jnp.float32
    ).astype(jnp.bfloat16)
    grad_heads = lax.map(
        attend_back,
        (
            split_heads[0],
            split_heads[1],
            split_heads[2],
            grad_mixed.reshape(seq_count, full_rows, heads_local, HEAD_DIM),
            log_total,
        ),
    )
    grad_projected = grad_heads.reshape(seq_count, 3, full_rows, local_width)
    grad_qkv = jnp.einsum(
        "tgd,gcte->cde", rows_one, grad_projected, preferred_element_type=jnp.float32
    )
    piece_rows = grad_projected
    grad_normed_one = lax.psum_scatter(
        jnp.einsum(
            "gcte,cde->tgd", piece_rows, qkv_weight, preferred_element_type=jnp.float32
        ).astype(jnp.bfloat16),
        "tensor",
        scatter_dimension=0,
        tiled=True,
    ).astype(jnp.float32)
    grad_input_norm, gain_one_grad, bias_one_grad = norm_back(
        grad_normed_one, normal_one, inverse_one, gain_one.astype(jnp.float32)
    )
    input_grad = (grad_hidden + grad_input_norm).astype(jnp.bfloat16)
    owned = (
        lax.psum_scatter(
            gain_one_grad.astype(jnp.bfloat16), "dp", scatter_dimension=0, tiled=True
        ).astype(jnp.float32),
        lax.psum_scatter(
            bias_one_grad.astype(jnp.bfloat16), "dp", scatter_dimension=0, tiled=True
        ).astype(jnp.float32),
        lax.psum_scatter(
            grad_qkv.astype(jnp.bfloat16), "dp", scatter_dimension=1, tiled=True
        ).astype(jnp.float32),
        lax.psum_scatter(
            grad_out.astype(jnp.bfloat16), "dp", scatter_dimension=1, tiled=True
        ).astype(jnp.float32),
        lax.psum_scatter(
            gain_two_grad.astype(jnp.bfloat16), "dp", scatter_dimension=0, tiled=True
        ).astype(jnp.float32),
        lax.psum_scatter(
            bias_two_grad.astype(jnp.bfloat16), "dp", scatter_dimension=0, tiled=True
        ).astype(jnp.float32),
        lax.psum_scatter(
            grad_up.astype(jnp.bfloat16), "dp", scatter_dimension=0, tiled=True
        ).astype(jnp.float32),
        lax.psum_scatter(
            grad_down.astype(jnp.bfloat16), "dp", scatter_dimension=1, tiled=True
        ).astype(jnp.float32),
    )
    norm_sums = lax.psum((owned[0], owned[1], owned[4], owned[5]), "tensor")
    return (
        block_out,
        input_grad,
        norm_sums[0],
        norm_sums[1],
        owned[2],
        owned[3],
        norm_sums[2],
        norm_sums[3],
        owned[6],
        owned[7],
    )


LOG2E = 1.4426950408889634
BLOCK = 256
BIG = 24 * 2**20
NT = (((1,), (1,)), ((), ()))
TN = (((0,), (0,)), ((), ()))
NN = (((1,), (0,)), ((), ()))


def mul(left, right, dims=NN):
    return lax.dot_general(left, right, dims, preferred_element_type=jnp.float32)


def fwd_kernel(q_ref, k_ref, v_ref, o_ref, lse_ref):
    length = q_ref.shape[0]
    scale = LOG2E * HEAD_DIM**-0.5
    block = min(BLOCK, length)
    keep = lax.broadcasted_iota(jnp.int32, (block, block), 1) <= lax.broadcasted_iota(
        jnp.int32, (block, block), 0
    )
    heads = q_ref.shape[1] // HEAD_DIM
    for i in range(length // block):
        rows = slice(i * block, (i + 1) * block)
        outs = []
        for h in range(heads):
            cols = slice(h * HEAD_DIM, (h + 1) * HEAD_DIM)
            q = q_ref[rows, cols]
            diag = jnp.where(keep, mul(q, k_ref[rows, cols], NT), -1e30)
            top = jnp.max(diag, axis=1, keepdims=True)
            if i > 0:
                past = mul(q, k_ref[: i * block, cols], NT)
                top = jnp.maximum(top, jnp.max(past, axis=1, keepdims=True))
            shift = top * scale
            w = jnp.exp2(diag * scale - shift)
            total = jnp.sum(w, axis=1, keepdims=True)
            out = mul(w.astype(jnp.bfloat16), v_ref[rows, cols])
            if i > 0:
                w = jnp.exp2(past * scale - shift)
                total = total + jnp.sum(w, axis=1, keepdims=True)
                out = out + mul(w.astype(jnp.bfloat16), v_ref[: i * block, cols])
            outs.append(out / total)
            lse = shift + jnp.log2(total)
            lse_ref[0, h : h + 1, rows] = jnp.broadcast_to(lse, (block, 128)).T[:1]
        o_ref[rows, :] = jnp.concatenate(outs, axis=1).astype(jnp.bfloat16)


def attend(qkv):
    length, width3 = qkv.shape
    width = width3 // 3
    pairs = width // 128
    return pl.pallas_call(
        fwd_kernel,
        grid=(pairs,),
        in_specs=[
            pl.BlockSpec((length, 128), lambda j: (0, j)),
            pl.BlockSpec((length, 128), lambda j: (0, pairs + j)),
            pl.BlockSpec((length, 128), lambda j: (0, 2 * pairs + j)),
        ],
        out_specs=[
            pl.BlockSpec((length, 128), lambda j: (0, j)),
            pl.BlockSpec((1, 8, length), lambda j: (j, 0, 0)),
        ],
        out_shape=[
            jax.ShapeDtypeStruct((length, width), jnp.bfloat16),
            jax.ShapeDtypeStruct((pairs, 8, length), jnp.float32),
        ],
        compiler_params=pltpu.CompilerParams(vmem_limit_bytes=BIG),
        cost_estimate=pl.CostEstimate(
            flops=length, bytes_accessed=length, transcendentals=0
        ),
    )(qkv, qkv, qkv)


def back_kernel(q_ref, k_ref, v_ref, do_ref, o_ref, lse_ref, dqkv_ref):
    length = q_ref.shape[0]
    width = dqkv_ref.shape[1] // 3
    factor = HEAD_DIM**-0.5
    scale = LOG2E * factor
    block = min(BLOCK, length)
    keep = lax.broadcasted_iota(jnp.int32, (block, block), 0) <= lax.broadcasted_iota(
        jnp.int32, (block, block), 1
    )
    count = length // block
    heads = q_ref.shape[1] // HEAD_DIM
    col = pl.program_id(0) * 128
    both = do_ref[...].astype(jnp.float32) * o_ref[...].astype(jnp.float32)
    both = both.T
    deltas = [
        jnp.sum(both[h * HEAD_DIM : (h + 1) * HEAD_DIM], axis=0, keepdims=True)
        for h in range(heads)
    ]
    dqs = [[None] * count for _ in range(heads)]
    for j in range(count):
        rows = slice(j * block, (j + 1) * block)
        dks, dvs = [], []
        for h in range(heads):
            cols = slice(h * HEAD_DIM, (h + 1) * HEAD_DIM)
            k, v = k_ref[rows, cols], v_ref[rows, cols]
            q, do = q_ref[j * block :, cols], do_ref[j * block :, cols]
            lse = lse_ref[0, h : h + 1, j * block :]
            w = jnp.exp2(mul(k, q, NT) * scale - lse)
            if j + 1 < count:
                w = jnp.concatenate([jnp.where(keep, w[:, :block], 0.0), w[:, block:]], axis=1)
            else:
                w = jnp.where(keep, w, 0.0)
            ds = (w * (mul(v, do, NT) - deltas[h][:, j * block :])).astype(jnp.bfloat16)
            dvs.append(mul(w.astype(jnp.bfloat16), do))
            dks.append(mul(ds, q) * factor)
            dq = mul(ds, k, TN)
            for i in range(j, count):
                part = dq[(i - j) * block : (i - j + 1) * block]
                dqs[h][i] = part if dqs[h][i] is None else dqs[h][i] + part
        dqkv_ref[rows, pl.ds(pl.multiple_of(width + col, 128), 128)] = jnp.concatenate(
            dks, axis=1
        ).astype(jnp.bfloat16)
        dqkv_ref[rows, pl.ds(pl.multiple_of(2 * width + col, 128), 128)] = jnp.concatenate(
            dvs, axis=1
        ).astype(jnp.bfloat16)
        dqkv_ref[rows, pl.ds(pl.multiple_of(col, 128), 128)] = (
            jnp.concatenate([dqs[h][j] for h in range(heads)], axis=1) * factor
        ).astype(jnp.bfloat16)


def attend_grad(qkv, grad_mixed, mixed, lse):
    length, width3 = qkv.shape
    width = width3 // 3
    pairs = width // 128
    return pl.pallas_call(
        back_kernel,
        grid=(pairs,),
        in_specs=[
            pl.BlockSpec((length, 128), lambda j: (0, j)),
            pl.BlockSpec((length, 128), lambda j: (0, pairs + j)),
            pl.BlockSpec((length, 128), lambda j: (0, 2 * pairs + j)),
            pl.BlockSpec((length, 128), lambda j: (0, j)),
            pl.BlockSpec((length, 128), lambda j: (0, j)),
            pl.BlockSpec((1, 8, length), lambda j: (j, 0, 0)),
        ],
        out_specs=pl.BlockSpec((length, width3), lambda j: (0, 0)),
        out_shape=jax.ShapeDtypeStruct((length, width3), jnp.bfloat16),
        compiler_params=pltpu.CompilerParams(vmem_limit_bytes=BIG),
        cost_estimate=pl.CostEstimate(
            flops=length, bytes_accessed=length, transcendentals=0
        ),
    )(qkv, qkv, qkv, grad_mixed, mixed, lse)


def swap_dp(array, size, mask):
    return lax.ppermute(array, "dp", [(i, i ^ mask) for i in range(size)])


def swap_tensor(array):
    return lax.ppermute(array, "tensor", [(0, 1), (1, 0)])


def add_low(left, right):
    return (left.astype(jnp.float32) + right.astype(jnp.float32)).astype(jnp.bfloat16)


def sum_kernel(count, pieces, *refs):
    out_ref = refs[-1]
    start = 0
    for p in range(pieces):
        end = start + refs[count + p].shape[0]
        total = mul(refs[0][...], refs[count + p][...], NT)
        for i in range(1, count):
            total = total + mul(refs[i][...], refs[count + i * pieces + p][...], NT)
        out_ref[:, start:end] = total
        start = end


def sum_products(lefts, rights, limit=BIG):
    rows, pieces = lefts[0].shape[0], len(rights[0])
    columns = sum(piece.shape[0] for piece in rights[0])
    flat = [piece for right in rights for piece in right]
    block = min(256, rows)
    return pl.pallas_call(
        functools.partial(sum_kernel, len(lefts), pieces),
        grid=(rows // block,),
        in_specs=[pl.BlockSpec((block, left.shape[1]), lambda i: (i, 0)) for left in lefts]
        + [
            pl.BlockSpec(piece.shape, lambda i: (0, 0), pipeline_mode=pl.Buffered(1)) for piece in flat
        ],
        out_specs=pl.BlockSpec((block, columns), lambda i: (i, 0)),
        out_shape=jax.ShapeDtypeStruct((rows, columns), jnp.float32),
        compiler_params=pltpu.CompilerParams(vmem_limit_bytes=limit),
        cost_estimate=tiny_cost(),
    )(*lefts, *flat)


def stack_rows(array, arrived):
    return jnp.concatenate([array, arrived], axis=0)


def low_half(array):
    return array[: array.shape[0] // 2]


def high_half(array):
    return array[array.shape[0] // 2 :]


def tiny_cost():
    return pl.CostEstimate(flops=1024, bytes_accessed=1024, transcendentals=0)


def row_kernel(rows_ref, columns_ref, *refs):
    out_ref, flipped = refs[-2:]

    @pl.when(pl.program_id(0) == 0)
    def _():
        flipped[...] = rows_ref[...].T

    block = out_ref.shape[0] // 2
    for i in range(2):
        part = slice(i * block, (i + 1) * block)
        out = mul(flipped[part, :], columns_ref[...])
        if len(refs) == 3:
            out = out + refs[0][part, :].astype(jnp.float32)
        out_ref[part, :] = out.astype(jnp.bfloat16)


def half_product(rows, columns, side, *arrived):
    depth, width = columns.shape
    half = rows.shape[1] // 2
    block = width // 4 if width >= 2048 else width // 2
    return pl.pallas_call(
        row_kernel,
        grid=(width // block,),
        in_specs=[
            pl.BlockSpec((depth, half), lambda j: (0, side)),
            pl.BlockSpec((depth, block), lambda j: (0, j)),
        ]
        + [pl.BlockSpec((half, block), lambda j: (0, j)) for _ in arrived],
        out_specs=pl.BlockSpec((half, block), lambda j: (0, j)),
        out_shape=jax.ShapeDtypeStruct((half, width), jnp.bfloat16),
        scratch_shapes=[pltpu.VMEM((half, depth), jnp.bfloat16)],
        compiler_params=pltpu.CompilerParams(vmem_limit_bytes=BIG),
        cost_estimate=tiny_cost(),
    )(rows, columns, *arrived)


def away_rows(rows, columns):
    return half_product(rows, columns, 1)


def kept_rows(rows, columns, arrived):
    return half_product(rows, columns, 0, arrived)


def two_part(rows, first_ref, second_ref):
    middle = first_ref.shape[0]
    return mul(rows[:, :middle], first_ref[...]) + mul(rows[:, middle:], second_ref[...])


def up_kernel(rows_ref, first_ref, second_ref, active_ref, slope_ref):
    rows = rows_ref.shape[0]
    block = min(256, rows)
    for i in range(rows // block):
        part = slice(i * block, (i + 1) * block)
        active, slope = gelu_both(two_part(rows_ref[part, :], first_ref, second_ref))
        active_ref[part, :] = active.astype(jnp.bfloat16)
        slope_ref[part, :] = slope.astype(jnp.bfloat16)


def back_up_kernel(rows_ref, first_ref, second_ref, slope_ref, out_ref):
    rows = rows_ref.shape[0]
    block = min(256, rows)
    for i in range(rows // block):
        part = slice(i * block, (i + 1) * block)
        out = two_part(rows_ref[part, :], first_ref, second_ref)
        out_ref[part, :] = (out * slope_ref[part, :].astype(jnp.float32)).astype(jnp.bfloat16)


def hidden_call(kernel, outputs, rows, weight, *others):
    count, depth = rows.shape
    width = weight[0].shape[1]
    block = min(512, width)
    shape = jax.ShapeDtypeStruct((count, width), jnp.bfloat16)
    spec = pl.BlockSpec((count, block), lambda j: (0, j))
    return pl.pallas_call(
        kernel,
        grid=(width // block,),
        in_specs=[pl.BlockSpec((count, depth), lambda j: (0, 0))]
        + [pl.BlockSpec((piece.shape[0], block), lambda j: (0, j)) for piece in weight]
        + [spec for _ in others],
        out_specs=[spec] * outputs,
        out_shape=[shape] * outputs,
        compiler_params=pltpu.CompilerParams(vmem_limit_bytes=BIG),
        cost_estimate=tiny_cost(),
    )(rows, *weight, *others)


def fold_dp(array, size, mask):
    return add_low(low_half(array), swap_dp(high_half(array), size, mask))


class Steps:
    def __init__(self):
        self.live = {}

    def __getattr__(self, name):
        return self.live[name]

    def put(self, **arrays):
        self.live.update(arrays)

    def drop(self, **names):
        for name in names:
            del self.live[name]

    def send(self, name, size, mask):
        self.live[name + "_in"] = swap_dp(self.live[name], size, mask)

    def merge(self, name):
        self.live[name] = stack_rows(self.live[name], self.live.pop(name + "_in"))

    def send_half(self, name, size, mask):
        whole = self.live[name]
        self.live[name], self.live[name + "_in"] = (
            low_half(whole), swap_dp(high_half(whole), size, mask)
        )

    def add(self, name):
        self.live[name] = add_low(self.live[name], self.live.pop(name + "_in"))

    def cut(self):
        names = list(self.live)
        arrays = lax.optimization_barrier(tuple(self.live[name] for name in names))
        self.live = dict(zip(names, arrays))


def norm_rows_grad(grad_in, normal, inverse, norm_gain):
    gain_grad = jnp.sum(grad_in * normal, axis=0, keepdims=True)
    bias_grad = jnp.sum(grad_in, axis=0, keepdims=True)
    scaled = grad_in * norm_gain
    first = jnp.mean(scaled, axis=-1, keepdims=True)
    second = jnp.mean(scaled * normal, axis=-1, keepdims=True)
    return (inverse * (scaled - first - normal * second), gain_grad, bias_grad)


def block_order(size, width):
    block = width // size
    here = lax.axis_index("dp")
    column = lax.broadcasted_iota(jnp.int32, (width, width), 1)
    place, inside = column // block, column % block
    source = here
    bit, value = size // 2, 1
    while bit >= 1:
        source = source ^ jnp.where((place // bit) % 2 == 1, value, 0)
        bit //= 2
        value *= 2
    row = lax.broadcasted_iota(jnp.int32, (width, width), 0)
    return (row == source * block + inside).astype(jnp.bfloat16)


def gelu_both(u):
    first = math.sqrt(2 / math.pi)
    third = 0.044715 * first
    square = u * u
    h = 0.5 * jnp.tanh(u * (first + third * square)) + 0.5
    slope = h + (h - h * h) * (u * (2 * first + 6 * third * square))
    return u * h, slope


def on_device_whole(
    size, tokens, d_out, ln1_gain, ln1_bias, w_qkv, w_out, ln2_gain, ln2_bias, w_up, w_down
):
    half_rows, _, width = tokens.shape
    first = lax.axis_index("tensor") == 0
    far, near = size // 2, size // 4

    def split(array):
        me = lax.axis_index("tensor")
        return (
            lax.dynamic_index_in_dim(array, me, 1, keepdims=False),
            lax.dynamic_index_in_dim(array, 1 - me, 1, keepdims=False),
        )

    def join(ours, arrived, order):
        rows = jnp.concatenate(
            [jnp.where(first, ours, arrived), jnp.where(first, arrived, ours)], axis=0
        )
        return mul(rows, order).astype(jnp.bfloat16)

    def reorder(rows, order):
        return mul(rows, order, NT).astype(jnp.bfloat16)

    def part(rows):
        low, high = rows[:half_rows], rows[half_rows:]
        return jnp.where(first, low, high), jnp.where(first, high, low)

    def place(ours, arrived):
        return jnp.stack(
            [jnp.where(first, ours, arrived), jnp.where(first, arrived, ours)], axis=1
        )

    def grow(array, mask):
        return stack_rows(array, swap_dp(array, size, mask))

    row_count, local_width = w_qkv.shape[1:]
    step = local_width // 2
    qkv_a, qkv_b = (
        w_qkv[:, :, p * step : (p + 1) * step].transpose(1, 0, 2).reshape(row_count, 3 * step)
        for p in range(2)
    )
    params = jnp.stack([ln1_gain, ln1_bias, ln2_gain, ln2_bias], axis=1)
    extra = 3 * step
    qkv_a = jnp.concatenate([qkv_a, jnp.pad(params, ((0, 0), (0, 128 - 4)))], axis=1)
    s = Steps()

    ours, away = split(tokens)
    arriving = swap_tensor(away)
    s.put(a=grow(qkv_a, far), b=grow(qkv_b, far))
    s.put(o=w_out.T, u=w_up, d=w_down.T, ours=ours, d_out=d_out)
    s.cut()
    s.put(a=grow(s.a, near), b=grow(s.b, near))
    s.cut()
    u_far = swap_dp(s.u, size, far)
    s.put(ay=grow(s.a, 2), o=grow(s.o, far))
    s.cut()
    ax = swap_tensor(s.a)
    a_core = swap_dp(s.ay, size, 1)
    s.put(b=grow(s.b, 2), o=grow(s.o, near), u=stack_rows(s.u, u_far))
    s.put(a_own=stack_rows(s.ay[:, :extra], a_core[:, :extra]))
    par = stack_rows(s.ay[:, extra:], a_core[:, extra:]).astype(jnp.float32).T
    order = block_order(size, width)
    s.put(x16=join(s.ours, arriving, order), ax=ax, order=order)
    gain_one, bias_one, gain_two, bias_two = (par[i : i + 1] for i in range(4))
    normed, normal, inverse = norm_rows(s.x16.astype(jnp.float32), gain_one, bias_one)
    s.put(n1=normed.astype(jnp.bfloat16), normal1=normal, inverse1=inverse)
    s.put(gain_one=gain_one, gain_two=gain_two, bias_two=bias_two)
    s.drop(a=0, ay=0, ours=0)
    s.cut()
    s.put(ox=swap_tensor(s.o), bx=swap_tensor(s.b))
    s.send("o", size, 2)
    s.send("u", size, near)
    b_own = grow(s.b, 1)
    s.put(ax=s.ax[:, :extra])
    s.send("ax", size, 2)
    qkv = mul(s.n1, s.a_own).astype(jnp.bfloat16)
    mixed, lse = attend(qkv)
    s.put(qkv0=qkv, mixed0=mixed, lse0=lse)
    qkv = mul(s.n1, b_own).astype(jnp.bfloat16)
    mixed, lse = attend(qkv)
    s.put(qkv1=qkv, mixed1=mixed, lse1=lse, b_own=b_own)
    s.drop(b=0)
    s.cut()
    s.merge("u")
    s.put(ux=swap_tensor(s.u))
    s.send("u", size, 2)
    s.send("ox", size, 2)
    s.send("d", size, far)
    s.merge("o")
    s.send("o", size, 1)
    s.merge("ax")
    a_oth, b_oth = grow(s.ax, 1), grow(s.bx, 1)
    qkv = mul(s.n1, a_oth).astype(jnp.bfloat16)
    mixed, lse = attend(qkv)
    s.put(qkv2=qkv, mixed2=mixed, lse2=lse)
    qkv = mul(s.n1, b_oth).astype(jnp.bfloat16)
    mixed, lse = attend(qkv)
    s.put(qkv3=qkv, mixed3=mixed, lse3=lse, a_oth=a_oth, b_oth=b_oth)
    s.drop(ax=0, bx=0)
    s.cut()
    ours, away = split(s.d_out)
    s.put(arrived=swap_tensor(away), ours=ours)
    s.send("ux", size, 2)
    s.merge("d")
    s.send("d", size, near)
    s.merge("u")
    s.merge("ox")
    s.merge("o")
    o_oth = grow(s.ox, 1)
    u_own = s.u, swap_dp(s.u, size, 1)
    mixed = jnp.concatenate([s.mixed0, s.mixed1, s.mixed2, s.mixed3], axis=1)
    out_all = jnp.concatenate([s.o, o_oth], axis=1)
    hidden = s.x16.astype(jnp.float32) + mul(mixed, out_all, NT)
    normed, normal, inverse = norm_rows(hidden, s.gain_two, s.bias_two)
    n2 = normed.astype(jnp.bfloat16)
    active, slope = hidden_call(up_kernel, 2, n2, u_own)
    s.put(active0=active, slope0=slope, u_own=u_own[0], u_own_b=u_own[1])
    s.put(mixed=mixed, out_all=out_all, hidden=hidden, n2=n2, normal2=normal, inverse2=inverse)
    s.drop(o=0, ox=0, x16=0, bias_two=0, u=0, d_out=0)
    s.cut()
    s.merge("d")
    s.put(dx=swap_tensor(s.d))
    s.send("d", size, 2)
    s.merge("ux")
    u_oth = s.ux, swap_dp(s.ux, size, 1)
    dy16 = join(s.ours, s.arrived, s.order)
    down0 = swap_dp(away_rows(dy16, s.active0), size, 1)
    active, slope = hidden_call(up_kernel, 2, s.n2, u_oth)
    s.put(active1=active, slope1=slope, u_oth=u_oth[0], u_oth_b=u_oth[1], dy16=dy16)
    down1 = swap_dp(away_rows(dy16, active), size, 1)
    s.drop(ux=0, ours=0, arrived=0)
    s.cut()
    s.send("dx", size, 2)
    s.merge("d")
    d_own = s.d, swap_dp(s.d, size, 1)
    s.put(down1=kept_rows(s.dy16, s.active1, down1), down0=kept_rows(s.dy16, s.active0, down0))
    (grad,) = hidden_call(back_up_kernel, 1, s.dy16, d_own, s.slope0)
    s.put(up_grad0=grad, d_own=d_own[0], d_own_b=d_own[1])
    up0 = swap_dp(away_rows(s.n2, grad), size, 1)
    s.drop(slope0=0, d=0)
    s.cut()
    s.put(down_h=high_half(s.down0), down_h_in=swap_tensor(high_half(s.down1)))
    s.put(down0=low_half(s.down0), down1=low_half(s.down1))
    s.merge("dx")
    d_oth = s.dx, swap_dp(s.dx, size, 1)
    s.put(up0=kept_rows(s.n2, s.up_grad0, up0))
    (grad,) = hidden_call(back_up_kernel, 1, s.dy16, d_oth, s.slope1)
    s.put(up_grad1=grad)
    up1 = swap_dp(away_rows(s.n2, grad), size, 1)
    s.put(block=sum_products([s.active0, s.active1], [(s.d_own, s.d_own_b), d_oth]))
    s.drop(slope1=0, dx=0, active0=0, active1=0, d_own=0, d_own_b=0)
    s.cut()
    s.put(down0_in=swap_tensor(s.down1))
    s.send_half("up0", size, 2)
    s.put(up1=kept_rows(s.n2, s.up_grad1, up1))
    rows = reorder((s.hidden + s.block).astype(jnp.bfloat16), s.order)
    ours, away = part(rows)
    s.put(ours=ours, away=away)
    s.put(grad_n2=sum_products([s.up_grad0, s.up_grad1], [(s.u_own, s.u_own_b), (s.u_oth, s.u_oth_b)]))
    s.drop(hidden=0, block=0, n2=0, down1=0, up_grad0=0, up_grad1=0, u_own=0, u_oth=0)
    s.drop(u_own_b=0, u_oth_b=0)
    s.cut()
    s.put(block_arrived=swap_tensor(s.away))
    s.send_half("up1", size, 2)
    grad_norm, gain_two_grad, bias_two_grad = norm_rows_grad(
        s.grad_n2, s.normal2, s.inverse2, s.gain_two
    )
    grad_hidden = s.dy16.astype(jnp.float32) + grad_norm
    low_hidden = grad_hidden.astype(jnp.bfloat16)
    s.put(gain_two_grad=gain_two_grad, bias_two_grad=bias_two_grad, grad_hidden=grad_hidden)
    grad_mixed = mul(low_hidden, s.out_all).astype(jnp.bfloat16)
    s.put(low_hidden=low_hidden, grad_mixed=grad_mixed)
    out0 = swap_dp(away_rows(low_hidden, s.mixed[:, :local_width]), size, 1)
    out1 = swap_dp(away_rows(low_hidden, s.mixed[:, local_width:]), size, 1)
    s.put(dqkv0=attend_grad(s.qkv0, grad_mixed[:, :step], s.mixed0, s.lse0))
    s.drop(grad_n2=0, away=0, normal2=0, inverse2=0, gain_two=0, out_all=0)
    s.drop(qkv0=0, mixed0=0, lse0=0)
    s.cut()
    s.add("up1")
    s.put(up0_x=swap_tensor(s.up1))
    s.add("down_h")
    s.put(down0_y=swap_dp(s.down_h, size, 2))
    s.put(out0=kept_rows(s.low_hidden, s.mixed[:, :local_width], out0))
    s.put(out1=kept_rows(s.low_hidden, s.mixed[:, local_width:], out1))
    a0 = swap_dp(away_rows(s.n1, s.dqkv0), size, 1)
    dqkv2 = attend_grad(s.qkv2, s.grad_mixed[:, 2 * step : 3 * step], s.mixed2, s.lse2)
    a1 = swap_dp(away_rows(s.n1, dqkv2), size, 1)
    dqkv1 = attend_grad(s.qkv1, s.grad_mixed[:, step : 2 * step], s.mixed1, s.lse1)
    s.put(dqkv1=dqkv1, dqkv2=dqkv2)
    s.add("up0")
    s.add("down0")
    s.drop(low_hidden=0, dy16=0, mixed=0, qkv2=0, mixed2=0, lse2=0, up1=0, down_h=0)
    s.drop(qkv1=0, mixed1=0, lse1=0)
    s.cut()

    def last_half(array):
        return low_half(array), swap_dp(high_half(array), size, far)

    def last_add(kept, arrived):
        return kept.astype(jnp.float32) + arrived.astype(jnp.float32)

    def last_fold(array):
        return last_add(*last_half(array))

    s.put(up0_in=s.up0_x, down0_in=s.down0_y)
    s.add("up0")
    s.add("down0")
    s.send_half("up0", size, near)
    s.send_half("down0", size, near)
    s.send_half("out0", size, 2)
    s.send_half("out1", size, 2)
    a1 = kept_rows(s.n1, s.dqkv2, a1)
    s.put(a0=kept_rows(s.n1, s.dqkv0, a0), a0_in=swap_tensor(a1))
    b0 = swap_dp(away_rows(s.n1, s.dqkv1), size, 1)
    dqkv3 = attend_grad(s.qkv3, s.grad_mixed[:, 3 * step :], s.mixed3, s.lse3)
    b1 = swap_dp(away_rows(s.n1, dqkv3), size, 1)
    s.put(dqkv3=dqkv3)
    s.drop(qkv3=0, mixed3=0, lse3=0, grad_mixed=0, up0_x=0, down0_y=0)
    s.cut()
    for name in ("up0", "down0", "out0", "out1", "a0"):
        s.add(name)
    b1 = kept_rows(s.n1, s.dqkv3, b1)
    s.put(b0=kept_rows(s.n1, s.dqkv1, b0), b1=b1)
    s.cut()
    s.put(b0_in=swap_tensor(s.b1))
    s.send_half("up0", size, far)
    s.send_half("down0", size, far)
    grad_n1 = sum_products(
        [s.dqkv0, s.dqkv1, s.dqkv2, s.dqkv3], [(s.a_own,), (s.b_own,), (s.a_oth,), (s.b_oth,)],
        56 * 2**20,
    )
    s.put(grad_n1=grad_n1)
    s.cut()
    s.put(out0_in=swap_tensor(s.out1))
    s.send_half("a0", size, 2)
    grad_norm, gain_one_grad, bias_one_grad = norm_rows_grad(
        s.grad_n1, s.normal1, s.inverse1, s.gain_one
    )
    rows = reorder((s.grad_hidden + grad_norm).astype(jnp.bfloat16), s.order)
    ours, away = part(rows)
    s.put(input_ours=ours, input_away=away)
    s.put(
        sums=jnp.concatenate(
            [gain_one_grad, bias_one_grad, s.gain_two_grad, s.bias_two_grad], axis=0
        )
    )
    s.drop(grad_n1=0, dqkv0=0, dqkv1=0, dqkv2=0, dqkv3=0, a_own=0, b_own=0, a_oth=0, b_oth=0, out1=0, b1=0)
    s.drop(n1=0, normal1=0, inverse1=0, gain_one=0, grad_hidden=0, order=0)
    s.drop(gain_two_grad=0, bias_two_grad=0)
    s.cut()

    def fold_sums(array, mask):
        middle = array.shape[1] // 2
        return array[:, :middle] + swap_dp(array[:, middle:], size, mask)

    for name in ("b0", "a0", "out0"):
        s.add(name)
    s.send_half("b0", size, 2)
    s.send_half("a0", size, near)
    s.send_half("out0", size, near)
    most = s.input_away.shape[0] // 2
    s.put(most=swap_tensor(s.input_away[:most]), rest=s.input_away[most:])
    s.put(grad_up=last_add(s.up0, s.up0_in), grad_down=last_add(s.down0, s.down0_in))
    s.put(sums=fold_sums(fold_sums(s.sums, 1), 2))
    s.put(block_out=place(s.ours, s.block_arrived))
    s.drop(ours=0, block_arrived=0, input_away=0, up0=0, down0=0, up0_in=0, down0_in=0)
    s.cut()
    for name in ("b0", "a0", "out0"):
        s.add(name)
    s.send_half("b0", size, near)
    s.send_half("a0", size, far)
    s.send_half("out0", size, far)
    s.put(rest=swap_tensor(s.rest), sums=fold_sums(fold_sums(s.sums, near), far))
    s.cut()
    s.add("b0")
    input_grad = place(s.input_ours, jnp.concatenate([s.most, s.rest], axis=0))
    grad_a, grad_out = last_add(s.a0, s.a0_in), last_add(s.out0, s.out0_in)
    grad_b = last_fold(s.b0)
    sums = s.sums + swap_tensor(s.sums)

    return (
        s.block_out,
        input_grad,
        sums[0],
        sums[1],
        jnp.concatenate(
            [g.reshape(row_count, 3, step).transpose(1, 0, 2) for g in (grad_a, grad_b)], axis=2
        ),
        grad_out.T,
        sums[2],
        sums[3],
        s.grad_up,
        s.grad_down.T,
    )


def solution(mesh):
    sizes = dict(mesh.shape)
    dp_size, tensor_size = sizes["dp"], sizes["tensor"]
    if tensor_size == 2 and dp_size == 16:
        body = functools.partial(on_device_whole, dp_size)
    else:
        body = on_device_shared
    placed = (
        P("tensor", "dp", None),
        P("tensor", "dp", None),
        P("dp"),
        P("dp"),
        P(None, "dp", "tensor"),
        P("tensor", "dp"),
        P("dp"),
        P("dp"),
        P("dp", "tensor"),
        P("tensor", "dp"),
    )
    return jax.shard_map(
        body,
        mesh=mesh,
        in_specs=placed,
        out_specs=(
            P("tensor", "dp", None),
            P("tensor", "dp", None),
            P("dp"),
            P("dp"),
            P(None, "dp", "tensor"),
            P("tensor", "dp"),
            P("dp"),
            P("dp"),
            P("dp", "tensor"),
            P("tensor", "dp"),
        ),
        check_vma=False,
    )
```

```python
import functools
import math

import jax
import jax.numpy as jnp
from jax import lax
from jax.experimental import pallas as pl
from jax.experimental.pallas import tpu as pltpu
from jax.sharding import PartitionSpec as P

HEAD_DIM = 64


EPSILON = 1e-05


def norm_rows(values, norm_gain, norm_bias):
    center = jnp.mean(values, axis=-1, keepdims=True)
    centered = values - center
    inverse = lax.rsqrt(jnp.mean(centered * centered, axis=-1, keepdims=True) + EPSILON)
    normal = centered * inverse
    return (normal * norm_gain + norm_bias, normal, inverse)


def norm_back(grad_in, normal, inverse, norm_gain):
    gain_grad = jnp.sum(grad_in * normal, axis=(0, 1))
    bias_grad = jnp.sum(grad_in, axis=(0, 1))
    scaled = grad_in * norm_gain
    first = jnp.mean(scaled, axis=-1, keepdims=True)
    second = jnp.mean(scaled * normal, axis=-1, keepdims=True)
    return (inverse * (scaled - first - normal * second), gain_grad, bias_grad)


def causal_mask(length):
    row_index = lax.broadcasted_iota(jnp.int32, (length, length), 0)
    column_index = lax.broadcasted_iota(jnp.int32, (length, length), 1)
    return column_index <= row_index


def attend_forward(triple):
    queries, key_rows, value_rows = triple
    scores = jnp.einsum(
        "qhd,khd->hqk", queries, key_rows, preferred_element_type=jnp.float32
    ) * HEAD_DIM ** (-0.5)
    scores = jnp.where(causal_mask(queries.shape[0]), scores, -1e30)
    row_max = jnp.max(scores, axis=-1, keepdims=True)
    weights = jnp.exp(scores - row_max)
    totals = jnp.sum(weights, axis=-1, keepdims=True)
    shares = (weights / totals).astype(jnp.bfloat16)
    mixed = jnp.einsum("hqk,khd->qhd", shares, value_rows, preferred_element_type=jnp.float32)
    return (mixed.astype(jnp.bfloat16), row_max + jnp.log(totals))


def attend_back(group):
    queries, key_rows, value_rows, grad_mixed, log_total = group
    factor = HEAD_DIM ** (-0.5)
    scores = (
        jnp.einsum("qhd,khd->hqk", queries, key_rows, preferred_element_type=jnp.float32) * factor
    )
    scores = jnp.where(causal_mask(queries.shape[0]), scores, -1e30)
    shares = jnp.exp(scores - log_total)
    grad_value = jnp.einsum(
        "hqk,qhd->khd", shares.astype(jnp.bfloat16), grad_mixed, preferred_element_type=jnp.float32
    )
    grad_shares = jnp.einsum(
        "qhd,khd->hqk", grad_mixed, value_rows, preferred_element_type=jnp.float32
    )
    inner = jnp.sum(shares * grad_shares, axis=-1, keepdims=True)
    grad_scores = (shares * (grad_shares - inner)).astype(jnp.bfloat16)
    grad_query = (
        jnp.einsum("hqk,khd->qhd", grad_scores, key_rows, preferred_element_type=jnp.float32)
        * factor
    )
    grad_key = (
        jnp.einsum("hqk,qhd->khd", grad_scores, queries, preferred_element_type=jnp.float32)
        * factor
    )
    return jnp.stack([grad_query, grad_key, grad_value]).astype(jnp.bfloat16)


def on_device_shared(tokens, d_out, ln1_gain, ln1_bias, w_qkv, w_out, ln2_gain, ln2_bias, w_up, w_down):
    local_rows, seq_count, width = tokens.shape
    gathered = (
        lax.all_gather(ln1_gain, "dp", axis=0, tiled=True),
        lax.all_gather(ln1_bias, "dp", axis=0, tiled=True),
        lax.all_gather(w_qkv, "dp", axis=1, tiled=True),
        lax.all_gather(w_out, "dp", axis=1, tiled=True),
        lax.all_gather(ln2_gain, "dp", axis=0, tiled=True),
        lax.all_gather(ln2_bias, "dp", axis=0, tiled=True),
        lax.all_gather(w_up, "dp", axis=0, tiled=True),
        lax.all_gather(w_down, "dp", axis=1, tiled=True),
    )
    gain_one, bias_one, qkv_weight, out_weight, gain_two, bias_two, up_weight, down_weight = (
        gathered
    )
    residual = tokens.astype(jnp.float32)
    normed_one, normal_one, inverse_one = norm_rows(
        residual, gain_one.astype(jnp.float32), bias_one.astype(jnp.float32)
    )
    low_one = normed_one.astype(jnp.bfloat16)
    rows_one = lax.all_gather(low_one, "tensor", axis=0, tiled=True)
    full_rows = rows_one.shape[0]
    projected = jnp.einsum(
        "tgd,cde->cgte", rows_one, qkv_weight, preferred_element_type=jnp.float32
    ).astype(jnp.bfloat16)
    local_width = projected.shape[3]
    heads_local = local_width // HEAD_DIM
    split_heads = projected.reshape(3, seq_count, full_rows, heads_local, HEAD_DIM)
    mixed, log_total = lax.map(attend_forward, (split_heads[0], split_heads[1], split_heads[2]))
    mixed = mixed.reshape(seq_count, full_rows, local_width)
    piece_rows = mixed
    hidden = residual + lax.psum_scatter(
        jnp.einsum(
            "gte,ed->tgd", piece_rows, out_weight, preferred_element_type=jnp.float32
        ).astype(jnp.bfloat16),
        "tensor",
        scatter_dimension=0,
        tiled=True,
    ).astype(jnp.float32)
    normed_two, normal_two, inverse_two = norm_rows(
        hidden, gain_two.astype(jnp.float32), bias_two.astype(jnp.float32)
    )
    low_two = normed_two.astype(jnp.bfloat16)
    rows_two = lax.all_gather(low_two, "tensor", axis=0, tiled=True)
    upward = jnp.einsum("tgd,df->tgf", rows_two, up_weight, preferred_element_type=jnp.float32)
    active = jax.nn.gelu(upward, approximate=True).astype(jnp.bfloat16)
    piece_rows = active
    block_sum = lax.psum_scatter(
        jnp.einsum(
            "tgf,fd->tgd", piece_rows, down_weight, preferred_element_type=jnp.float32
        ).astype(jnp.bfloat16),
        "tensor",
        scatter_dimension=0,
        tiled=True,
    ).astype(jnp.float32)
    block_out = (hidden + block_sum).astype(jnp.bfloat16)
    grad_rows = lax.all_gather(d_out, "tensor", axis=0, tiled=True)
    grad_down = jnp.einsum("tgf,tgd->fd", active, grad_rows, preferred_element_type=jnp.float32)
    grad_active = jnp.einsum(
        "tgd,fd->tgf", grad_rows, down_weight, preferred_element_type=jnp.float32
    )
    gelu_pull = jax.vjp(lambda inner: jax.nn.gelu(inner, approximate=True), upward)[1]
    grad_upward = gelu_pull(grad_active)[0].astype(jnp.bfloat16)
    grad_up = jnp.einsum("tgd,tgf->df", rows_two, grad_upward, preferred_element_type=jnp.float32)
    piece_rows = grad_upward
    grad_normed_two = lax.psum_scatter(
        jnp.einsum("tgf,df->tgd", piece_rows, up_weight, preferred_element_type=jnp.float32).astype(
            jnp.bfloat16
        ),
        "tensor",
        scatter_dimension=0,
        tiled=True,
    ).astype(jnp.float32)
    grad_hidden_norm, gain_two_grad, bias_two_grad = norm_back(
        grad_normed_two, normal_two, inverse_two, gain_two.astype(jnp.float32)
    )
    grad_hidden = d_out.astype(jnp.float32) + grad_hidden_norm
    low_hidden = grad_hidden.astype(jnp.bfloat16)
    hidden_rows = lax.all_gather(low_hidden, "tensor", axis=0, tiled=True)
    grad_out = jnp.einsum("gte,tgd->ed", mixed, hidden_rows, preferred_element_type=jnp.float32)
    grad_mixed = jnp.einsum(
        "tgd,ed->gte", hidden_rows, out_weight, preferred_element_type=jnp.float32
    ).astype(jnp.bfloat16)
    grad_heads = lax.map(
        attend_back,
        (
            split_heads[0],
            split_heads[1],
            split_heads[2],
            grad_mixed.reshape(seq_count, full_rows, heads_local, HEAD_DIM),
            log_total,
        ),
    )
    grad_projected = grad_heads.reshape(seq_count, 3, full_rows, local_width)
    grad_qkv = jnp.einsum(
        "tgd,gcte->cde", rows_one, grad_projected, preferred_element_type=jnp.float32
    )
    piece_rows = grad_projected
    grad_normed_one = lax.psum_scatter(
        jnp.einsum(
            "gcte,cde->tgd", piece_rows, qkv_weight, preferred_element_type=jnp.float32
        ).astype(jnp.bfloat16),
        "tensor",
        scatter_dimension=0,
        tiled=True,
    ).astype(jnp.float32)
    grad_input_norm, gain_one_grad, bias_one_grad = norm_back(
        grad_normed_one, normal_one, inverse_one, gain_one.astype(jnp.float32)
    )
    input_grad = (grad_hidden + grad_input_norm).astype(jnp.bfloat16)
    owned = (
        lax.psum_scatter(
            gain_one_grad.astype(jnp.bfloat16), "dp", scatter_dimension=0, tiled=True
        ).astype(jnp.float32),
        lax.psum_scatter(
            bias_one_grad.astype(jnp.bfloat16), "dp", scatter_dimension=0, tiled=True
        ).astype(jnp.float32),
        lax.psum_scatter(
            grad_qkv.astype(jnp.bfloat16), "dp", scatter_dimension=1, tiled=True
        ).astype(jnp.float32),
        lax.psum_scatter(
            grad_out.astype(jnp.bfloat16), "dp", scatter_dimension=1, tiled=True
        ).astype(jnp.float32),
        lax.psum_scatter(
            gain_two_grad.astype(jnp.bfloat16), "dp", scatter_dimension=0, tiled=True
        ).astype(jnp.float32),
        lax.psum_scatter(
            bias_two_grad.astype(jnp.bfloat16), "dp", scatter_dimension=0, tiled=True
        ).astype(jnp.float32),
        lax.psum_scatter(
            grad_up.astype(jnp.bfloat16), "dp", scatter_dimension=0, tiled=True
        ).astype(jnp.float32),
        lax.psum_scatter(
            grad_down.astype(jnp.bfloat16), "dp", scatter_dimension=1, tiled=True
        ).astype(jnp.float32),
    )
    norm_sums = lax.psum((owned[0], owned[1], owned[4], owned[5]), "tensor")
    return (
        block_out,
        input_grad,
        norm_sums[0],
        norm_sums[1],
        owned[2],
        owned[3],
        norm_sums[2],
        norm_sums[3],
        owned[6],
        owned[7],
    )


LOG2E = 1.4426950408889634
BLOCK = 256
BIG = 18 * 2**20
NT = (((1,), (1,)), ((), ()))
TN = (((0,), (0,)), ((), ()))
NN = (((1,), (0,)), ((), ()))


def mul(left, right, dims=NN):
    return lax.dot_general(left, right, dims, preferred_element_type=jnp.float32)


def fwd_kernel(q_ref, k_ref, v_ref, o_ref, lse_ref):
    length = q_ref.shape[0]
    scale = LOG2E * HEAD_DIM**-0.5
    block = min(BLOCK, length)
    keep = lax.broadcasted_iota(jnp.int32, (block, block), 1) <= lax.broadcasted_iota(
        jnp.int32, (block, block), 0
    )
    heads = q_ref.shape[1] // HEAD_DIM
    for i in range(length // block):
        rows = slice(i * block, (i + 1) * block)
        outs = []
        for h in range(heads):
            cols = slice(h * HEAD_DIM, (h + 1) * HEAD_DIM)
            q = q_ref[rows, cols]
            diag = jnp.where(keep, mul(q, k_ref[rows, cols], NT), -1e30)
            top = jnp.max(diag, axis=1, keepdims=True)
            if i > 0:
                past = mul(q, k_ref[: i * block, cols], NT)
                top = jnp.maximum(top, jnp.max(past, axis=1, keepdims=True))
            shift = top * scale
            w = jnp.exp2(diag * scale - shift)
            total = jnp.sum(w, axis=1, keepdims=True)
            out = mul(w.astype(jnp.bfloat16), v_ref[rows, cols])
            if i > 0:
                w = jnp.exp2(past * scale - shift)
                total = total + jnp.sum(w, axis=1, keepdims=True)
                out = out + mul(w.astype(jnp.bfloat16), v_ref[: i * block, cols])
            outs.append(out / total)
            lse = shift + jnp.log2(total)
            lse_ref[0, h : h + 1, rows] = jnp.broadcast_to(lse, (block, 128)).T[:1]
        o_ref[rows, :] = jnp.concatenate(outs, axis=1).astype(jnp.bfloat16)


def attend(qkv):
    length, width3 = qkv.shape
    width = width3 // 3
    pairs = width // 128
    return pl.pallas_call(
        fwd_kernel,
        grid=(pairs,),
        in_specs=[
            pl.BlockSpec((length, 128), lambda j: (0, j)),
            pl.BlockSpec((length, 128), lambda j: (0, pairs + j)),
            pl.BlockSpec((length, 128), lambda j: (0, 2 * pairs + j)),
        ],
        out_specs=[
            pl.BlockSpec((length, 128), lambda j: (0, j)),
            pl.BlockSpec((1, 8, length), lambda j: (j, 0, 0)),
        ],
        out_shape=[
            jax.ShapeDtypeStruct((length, width), jnp.bfloat16),
            jax.ShapeDtypeStruct((pairs, 8, length), jnp.float32),
        ],
        compiler_params=pltpu.CompilerParams(vmem_limit_bytes=BIG),
        cost_estimate=pl.CostEstimate(
            flops=length, bytes_accessed=length, transcendentals=0
        ),
    )(qkv, qkv, qkv)


def back_kernel(q_ref, k_ref, v_ref, do_ref, o_ref, lse_ref, dqkv_ref):
    length = q_ref.shape[0]
    width = dqkv_ref.shape[1] // 3
    factor = HEAD_DIM**-0.5
    scale = LOG2E * factor
    block = min(BLOCK, length)
    keep = lax.broadcasted_iota(jnp.int32, (block, block), 0) <= lax.broadcasted_iota(
        jnp.int32, (block, block), 1
    )
    count = length // block
    heads = q_ref.shape[1] // HEAD_DIM
    col = pl.program_id(0) * 128
    both = do_ref[...].astype(jnp.float32) * o_ref[...].astype(jnp.float32)
    both = both.T
    deltas = [
        jnp.sum(both[h * HEAD_DIM : (h + 1) * HEAD_DIM], axis=0, keepdims=True)
        for h in range(heads)
    ]
    dqs = [[None] * count for _ in range(heads)]
    for j in range(count):
        rows = slice(j * block, (j + 1) * block)
        dks, dvs = [], []
        for h in range(heads):
            cols = slice(h * HEAD_DIM, (h + 1) * HEAD_DIM)
            k, v = k_ref[rows, cols], v_ref[rows, cols]
            q, do = q_ref[j * block :, cols], do_ref[j * block :, cols]
            lse = lse_ref[0, h : h + 1, j * block :]
            w = jnp.exp2(mul(k, q, NT) * scale - lse)
            if j + 1 < count:
                w = jnp.concatenate([jnp.where(keep, w[:, :block], 0.0), w[:, block:]], axis=1)
            else:
                w = jnp.where(keep, w, 0.0)
            ds = (w * (mul(v, do, NT) - deltas[h][:, j * block :])).astype(jnp.bfloat16)
            dvs.append(mul(w.astype(jnp.bfloat16), do))
            dks.append(mul(ds, q) * factor)
            dq = mul(ds, k, TN)
            for i in range(j, count):
                part = dq[(i - j) * block : (i - j + 1) * block]
                dqs[h][i] = part if dqs[h][i] is None else dqs[h][i] + part
        dqkv_ref[rows, pl.ds(pl.multiple_of(width + col, 128), 128)] = jnp.concatenate(
            dks, axis=1
        ).astype(jnp.bfloat16)
        dqkv_ref[rows, pl.ds(pl.multiple_of(2 * width + col, 128), 128)] = jnp.concatenate(
            dvs, axis=1
        ).astype(jnp.bfloat16)
        dqkv_ref[rows, pl.ds(pl.multiple_of(col, 128), 128)] = (
            jnp.concatenate([dqs[h][j] for h in range(heads)], axis=1) * factor
        ).astype(jnp.bfloat16)


def attend_grad(qkv, grad_mixed, mixed, lse):
    length, width3 = qkv.shape
    width = width3 // 3
    pairs = width // 128
    return pl.pallas_call(
        back_kernel,
        grid=(pairs,),
        in_specs=[
            pl.BlockSpec((length, 128), lambda j: (0, j)),
            pl.BlockSpec((length, 128), lambda j: (0, pairs + j)),
            pl.BlockSpec((length, 128), lambda j: (0, 2 * pairs + j)),
            pl.BlockSpec((length, 128), lambda j: (0, j)),
            pl.BlockSpec((length, 128), lambda j: (0, j)),
            pl.BlockSpec((1, 8, length), lambda j: (j, 0, 0)),
        ],
        out_specs=pl.BlockSpec((length, width3), lambda j: (0, 0)),
        out_shape=jax.ShapeDtypeStruct((length, width3), jnp.bfloat16),
        compiler_params=pltpu.CompilerParams(vmem_limit_bytes=BIG),
        cost_estimate=pl.CostEstimate(
            flops=length, bytes_accessed=length, transcendentals=0
        ),
    )(qkv, qkv, qkv, grad_mixed, mixed, lse)


def swap_dp(array, size, mask):
    return lax.ppermute(array, "dp", [(i, i ^ mask) for i in range(size)])


def swap_tensor(array):
    return lax.ppermute(array, "tensor", [(0, 1), (1, 0)])


def add_low(left, right):
    return (left.astype(jnp.float32) + right.astype(jnp.float32)).astype(jnp.bfloat16)


def sum_kernel(count, pieces, *refs):
    out_ref = refs[-1]
    start = 0
    for p in range(pieces):
        end = start + refs[count + p].shape[0]
        total = mul(refs[0][...], refs[count + p][...], NT)
        for i in range(1, count):
            total = total + mul(refs[i][...], refs[count + i * pieces + p][...], NT)
        out_ref[:, start:end] = total
        start = end


def sum_products(lefts, rights, limit=BIG):
    rows, pieces = lefts[0].shape[0], len(rights[0])
    columns = sum(piece.shape[0] for piece in rights[0])
    flat = [piece for right in rights for piece in right]
    block = min(256, rows)
    return pl.pallas_call(
        functools.partial(sum_kernel, len(lefts), pieces),
        grid=(rows // block,),
        in_specs=[pl.BlockSpec((block, left.shape[1]), lambda i: (i, 0)) for left in lefts]
        + [
            pl.BlockSpec(piece.shape, lambda i: (0, 0), pipeline_mode=pl.Buffered(1)) for piece in flat
        ],
        out_specs=pl.BlockSpec((block, columns), lambda i: (i, 0)),
        out_shape=jax.ShapeDtypeStruct((rows, columns), jnp.float32),
        compiler_params=pltpu.CompilerParams(vmem_limit_bytes=limit),
        cost_estimate=tiny_cost(),
    )(*lefts, *flat)


def stack_rows(array, arrived):
    return jnp.concatenate([array, arrived], axis=0)


def low_half(array):
    return array[: array.shape[0] // 2]


def high_half(array):
    return array[array.shape[0] // 2 :]


def tiny_cost():
    return pl.CostEstimate(flops=1024, bytes_accessed=1024, transcendentals=0)


def row_kernel(rows_ref, columns_ref, *refs):
    out_ref, flipped = refs[-2:]

    @pl.when(pl.program_id(0) == 0)
    def _():
        flipped[...] = rows_ref[...].T

    block = out_ref.shape[0] // 2
    for i in range(2):
        part = slice(i * block, (i + 1) * block)
        out = mul(flipped[part, :], columns_ref[...])
        if len(refs) == 3:
            out = out + refs[0][part, :].astype(jnp.float32)
        out_ref[part, :] = out.astype(jnp.bfloat16)


def half_product(rows, columns, side, *arrived):
    depth, width = columns.shape
    half = rows.shape[1] // 2
    block = width // 4 if width >= 2048 else width // 2
    return pl.pallas_call(
        row_kernel,
        grid=(width // block,),
        in_specs=[
            pl.BlockSpec((depth, half), lambda j: (0, side)),
            pl.BlockSpec((depth, block), lambda j: (0, j)),
        ]
        + [pl.BlockSpec((half, block), lambda j: (0, j)) for _ in arrived],
        out_specs=pl.BlockSpec((half, block), lambda j: (0, j)),
        out_shape=jax.ShapeDtypeStruct((half, width), jnp.bfloat16),
        scratch_shapes=[pltpu.VMEM((half, depth), jnp.bfloat16)],
        compiler_params=pltpu.CompilerParams(vmem_limit_bytes=BIG),
        cost_estimate=tiny_cost(),
    )(rows, columns, *arrived)


def away_rows(rows, columns):
    return half_product(rows, columns, 1)


def kept_rows(rows, columns, arrived):
    return half_product(rows, columns, 0, arrived)


def two_part(rows, first_ref, second_ref):
    middle = first_ref.shape[0]
    return mul(rows[:, :middle], first_ref[...]) + mul(rows[:, middle:], second_ref[...])


def up_kernel(rows_ref, first_ref, second_ref, active_ref, slope_ref):
    rows = rows_ref.shape[0]
    block = min(256, rows)
    for i in range(rows // block):
        part = slice(i * block, (i + 1) * block)
        active, slope = gelu_both(two_part(rows_ref[part, :], first_ref, second_ref))
        active_ref[part, :] = active.astype(jnp.bfloat16)
        slope_ref[part, :] = slope.astype(jnp.bfloat16)


def back_up_kernel(rows_ref, first_ref, second_ref, slope_ref, out_ref):
    rows = rows_ref.shape[0]
    block = min(256, rows)
    for i in range(rows // block):
        part = slice(i * block, (i + 1) * block)
        out = two_part(rows_ref[part, :], first_ref, second_ref)
        out_ref[part, :] = (out * slope_ref[part, :].astype(jnp.float32)).astype(jnp.bfloat16)


def hidden_call(kernel, outputs, rows, weight, *others):
    count, depth = rows.shape
    width = weight[0].shape[1]
    block = min(512, width)
    shape = jax.ShapeDtypeStruct((count, width), jnp.bfloat16)
    spec = pl.BlockSpec((count, block), lambda j: (0, j))
    return pl.pallas_call(
        kernel,
        grid=(width // block,),
        in_specs=[pl.BlockSpec((count, depth), lambda j: (0, 0))]
        + [pl.BlockSpec((piece.shape[0], block), lambda j: (0, j)) for piece in weight]
        + [spec for _ in others],
        out_specs=[spec] * outputs,
        out_shape=[shape] * outputs,
        compiler_params=pltpu.CompilerParams(vmem_limit_bytes=BIG),
        cost_estimate=tiny_cost(),
    )(rows, *weight, *others)


def fold_dp(array, size, mask):
    return add_low(low_half(array), swap_dp(high_half(array), size, mask))


class Steps:
    def __init__(self):
        self.live = {}

    def __getattr__(self, name):
        return self.live[name]

    def put(self, **arrays):
        self.live.update(arrays)

    def drop(self, **names):
        for name in names:
            del self.live[name]

    def send(self, name, size, mask):
        self.live[name + "_in"] = swap_dp(self.live[name], size, mask)

    def merge(self, name):
        self.live[name] = stack_rows(self.live[name], self.live.pop(name + "_in"))

    def send_half(self, name, size, mask):
        whole = self.live[name]
        self.live[name], self.live[name + "_in"] = (
            low_half(whole), swap_dp(high_half(whole), size, mask)
        )

    def add(self, name):
        self.live[name] = add_low(self.live[name], self.live.pop(name + "_in"))

    def cut(self):
        names = list(self.live)
        arrays = lax.optimization_barrier(tuple(self.live[name] for name in names))
        self.live = dict(zip(names, arrays))


def norm_rows_grad(grad_in, normal, inverse, norm_gain):
    gain_grad = jnp.sum(grad_in * normal, axis=0, keepdims=True)
    bias_grad = jnp.sum(grad_in, axis=0, keepdims=True)
    scaled = grad_in * norm_gain
    first = jnp.mean(scaled, axis=-1, keepdims=True)
    second = jnp.mean(scaled * normal, axis=-1, keepdims=True)
    return (inverse * (scaled - first - normal * second), gain_grad, bias_grad)


def block_order(size, width):
    block = width // size
    here = lax.axis_index("dp")
    column = lax.broadcasted_iota(jnp.int32, (width, width), 1)
    place, inside = column // block, column % block
    source = here
    bit, value = size // 2, 1
    while bit >= 1:
        source = source ^ jnp.where((place // bit) % 2 == 1, value, 0)
        bit //= 2
        value *= 2
    row = lax.broadcasted_iota(jnp.int32, (width, width), 0)
    return (row == source * block + inside).astype(jnp.bfloat16)


def gelu_both(u):
    first = math.sqrt(2 / math.pi)
    third = 0.044715 * first
    square = u * u
    h = 0.5 * jnp.tanh(u * (first + third * square)) + 0.5
    slope = h + (h - h * h) * (u * (2 * first + 6 * third * square))
    return u * h, slope


def on_device_whole(
    size, tokens, d_out, ln1_gain, ln1_bias, w_qkv, w_out, ln2_gain, ln2_bias, w_up, w_down
):
    half_rows, _, width = tokens.shape
    first = lax.axis_index("tensor") == 0
    far, near = size // 2, size // 4

    def split(array):
        me = lax.axis_index("tensor")
        return (
            lax.dynamic_index_in_dim(array, me, 1, keepdims=False),
            lax.dynamic_index_in_dim(array, 1 - me, 1, keepdims=False),
        )

    def join(ours, arrived, order):
        rows = jnp.concatenate(
            [jnp.where(first, ours, arrived), jnp.where(first, arrived, ours)], axis=0
        )
        return mul(rows, order).astype(jnp.bfloat16)

    def reorder(rows, order):
        return mul(rows, order, NT).astype(jnp.bfloat16)

    def part(rows):
        low, high = rows[:half_rows], rows[half_rows:]
        return jnp.where(first, low, high), jnp.where(first, high, low)

    def place(ours, arrived):
        return jnp.stack(
            [jnp.where(first, ours, arrived), jnp.where(first, arrived, ours)], axis=1
        )

    def grow(array, mask):
        return stack_rows(array, swap_dp(array, size, mask))

    row_count, local_width = w_qkv.shape[1:]
    step = local_width // 2
    qkv_a, qkv_b = (
        w_qkv[:, :, p * step : (p + 1) * step].transpose(1, 0, 2).reshape(row_count, 3 * step)
        for p in range(2)
    )
    params = jnp.stack([ln1_gain, ln1_bias, ln2_gain, ln2_bias], axis=1)
    extra = 3 * step
    qkv_a = jnp.concatenate([qkv_a, jnp.pad(params, ((0, 0), (0, 128 - 4)))], axis=1)
    s = Steps()

    ours, away = split(tokens)
    arriving = swap_tensor(away)
    s.put(a=grow(qkv_a, far), b=grow(qkv_b, far))
    s.put(o=w_out.T, u=w_up, d=w_down.T, ours=ours, d_out=d_out)
    s.cut()
    s.put(a=grow(s.a, near), b=grow(s.b, near))
    s.cut()
    u_far = swap_dp(s.u, size, far)
    s.put(ay=grow(s.a, 2), o=grow(s.o, far))
    s.cut()
    ax = swap_tensor(s.a)
    a_core = swap_dp(s.ay, size, 1)
    s.put(b=grow(s.b, 2), o=grow(s.o, near), u=stack_rows(s.u, u_far))
    s.put(a_own=stack_rows(s.ay[:, :extra], a_core[:, :extra]))
    par = stack_rows(s.ay[:, extra:], a_core[:, extra:]).astype(jnp.float32).T
    order = block_order(size, width)
    s.put(x16=join(s.ours, arriving, order), ax=ax, order=order)
    gain_one, bias_one, gain_two, bias_two = (par[i : i + 1] for i in range(4))
    normed, normal, inverse = norm_rows(s.x16.astype(jnp.float32), gain_one, bias_one)
    s.put(n1=normed.astype(jnp.bfloat16), normal1=normal, inverse1=inverse)
    s.put(gain_one=gain_one, gain_two=gain_two, bias_two=bias_two)
    s.drop(a=0, ay=0, ours=0)
    s.cut()
    s.put(ox=swap_tensor(s.o), bx=swap_tensor(s.b))
    s.send("o", size, 2)
    s.send("u", size, near)
    b_own = grow(s.b, 1)
    s.put(ax=s.ax[:, :extra])
    s.send("ax", size, 2)
    qkv = mul(s.n1, s.a_own).astype(jnp.bfloat16)
    mixed, lse = attend(qkv)
    s.put(qkv0=qkv, mixed0=mixed, lse0=lse)
    qkv = mul(s.n1, b_own).astype(jnp.bfloat16)
    mixed, lse = attend(qkv)
    s.put(qkv1=qkv, mixed1=mixed, lse1=lse, b_own=b_own)
    s.drop(b=0)
    s.cut()
    s.merge("u")
    s.put(ux=swap_tensor(s.u))
    s.send("u", size, 2)
    s.send("ox", size, 2)
    s.send("d", size, far)
    s.merge("o")
    s.send("o", size, 1)
    s.merge("ax")
    a_oth, b_oth = grow(s.ax, 1), grow(s.bx, 1)
    qkv = mul(s.n1, a_oth).astype(jnp.bfloat16)
    mixed, lse = attend(qkv)
    s.put(qkv2=qkv, mixed2=mixed, lse2=lse)
    qkv = mul(s.n1, b_oth).astype(jnp.bfloat16)
    mixed, lse = attend(qkv)
    s.put(qkv3=qkv, mixed3=mixed, lse3=lse, a_oth=a_oth, b_oth=b_oth)
    s.drop(ax=0, bx=0)
    s.cut()
    ours, away = split(s.d_out)
    s.put(arrived=swap_tensor(away), ours=ours)
    s.send("ux", size, 2)
    s.merge("d")
    s.send("d", size, near)
    s.merge("u")
    s.merge("ox")
    s.merge("o")
    o_oth = grow(s.ox, 1)
    u_own = s.u, swap_dp(s.u, size, 1)
    mixed = jnp.concatenate([s.mixed0, s.mixed1, s.mixed2, s.mixed3], axis=1)
    out_all = jnp.concatenate([s.o, o_oth], axis=1)
    hidden = s.x16.astype(jnp.float32) + mul(mixed, out_all, NT)
    normed, normal, inverse = norm_rows(hidden, s.gain_two, s.bias_two)
    n2 = normed.astype(jnp.bfloat16)
    active, slope = hidden_call(up_kernel, 2, n2, u_own)
    s.put(active0=active, slope0=slope, u_own=u_own[0], u_own_b=u_own[1])
    s.put(mixed=mixed, out_all=out_all, hidden=hidden, n2=n2, normal2=normal, inverse2=inverse)
    s.drop(o=0, ox=0, x16=0, bias_two=0, u=0, d_out=0)
    s.cut()
    s.merge("d")
    s.put(dx=swap_tensor(s.d))
    s.send("d", size, 2)
    s.merge("ux")
    u_oth = s.ux, swap_dp(s.ux, size, 1)
    dy16 = join(s.ours, s.arrived, s.order)
    down0 = swap_dp(away_rows(dy16, s.active0), size, 1)
    active, slope = hidden_call(up_kernel, 2, s.n2, u_oth)
    s.put(active1=active, slope1=slope, u_oth=u_oth[0], u_oth_b=u_oth[1], dy16=dy16)
    down1 = swap_dp(away_rows(dy16, active), size, 1)
    s.drop(ux=0, ours=0, arrived=0)
    s.cut()
    s.send("dx", size, 2)
    s.merge("d")
    d_own = s.d, swap_dp(s.d, size, 1)
    s.put(down1=kept_rows(s.dy16, s.active1, down1), down0=kept_rows(s.dy16, s.active0, down0))
    (grad,) = hidden_call(back_up_kernel, 1, s.dy16, d_own, s.slope0)
    s.put(up_grad0=grad, block=sum_products([s.active0], [d_own]))
    up0 = swap_dp(away_rows(s.n2, grad), size, 1)
    s.drop(slope0=0, d=0)
    s.cut()
    s.put(down_h=high_half(s.down0), down_h_in=swap_tensor(high_half(s.down1)))
    s.put(down0=low_half(s.down0), down1=low_half(s.down1))
    s.merge("dx")
    d_oth = s.dx, swap_dp(s.dx, size, 1)
    s.put(up0=kept_rows(s.n2, s.up_grad0, up0))
    (grad,) = hidden_call(back_up_kernel, 1, s.dy16, d_oth, s.slope1)
    s.put(up_grad1=grad)
    up1 = swap_dp(away_rows(s.n2, grad), size, 1)
    s.put(block_oth=sum_products([s.active1], [d_oth]))
    s.drop(slope1=0, dx=0, active0=0, active1=0)
    s.cut()
    s.put(down0_in=swap_tensor(s.down1))
    s.send_half("up0", size, 2)
    s.put(up1=kept_rows(s.n2, s.up_grad1, up1))
    rows = reorder((s.hidden + s.block + s.block_oth).astype(jnp.bfloat16), s.order)
    ours, away = part(rows)
    s.put(ours=ours, away=away)
    s.put(grad_n2=sum_products([s.up_grad0, s.up_grad1], [(s.u_own, s.u_own_b), (s.u_oth, s.u_oth_b)]))
    s.drop(hidden=0, block=0, block_oth=0, n2=0, down1=0, up_grad0=0, up_grad1=0, u_own=0, u_oth=0)
    s.drop(u_own_b=0, u_oth_b=0)
    s.cut()
    s.put(block_arrived=swap_tensor(s.away))
    s.send_half("up1", size, 2)
    grad_norm, gain_two_grad, bias_two_grad = norm_rows_grad(
        s.grad_n2, s.normal2, s.inverse2, s.gain_two
    )
    grad_hidden = s.dy16.astype(jnp.float32) + grad_norm
    low_hidden = grad_hidden.astype(jnp.bfloat16)
    s.put(gain_two_grad=gain_two_grad, bias_two_grad=bias_two_grad, grad_hidden=grad_hidden)
    grad_mixed = mul(low_hidden, s.out_all).astype(jnp.bfloat16)
    s.put(low_hidden=low_hidden, grad_mixed=grad_mixed)
    out0 = swap_dp(away_rows(low_hidden, s.mixed[:, :local_width]), size, 1)
    out1 = swap_dp(away_rows(low_hidden, s.mixed[:, local_width:]), size, 1)
    s.put(dqkv0=attend_grad(s.qkv0, grad_mixed[:, :step], s.mixed0, s.lse0))
    s.drop(grad_n2=0, away=0, normal2=0, inverse2=0, gain_two=0, out_all=0)
    s.drop(qkv0=0, mixed0=0, lse0=0)
    s.cut()
    s.add("up1")
    s.put(up0_x=swap_tensor(s.up1))
    s.add("down_h")
    s.put(down0_y=swap_dp(s.down_h, size, 2))
    s.put(out0=kept_rows(s.low_hidden, s.mixed[:, :local_width], out0))
    s.put(out1=kept_rows(s.low_hidden, s.mixed[:, local_width:], out1))
    a0 = swap_dp(away_rows(s.n1, s.dqkv0), size, 1)
    dqkv2 = attend_grad(s.qkv2, s.grad_mixed[:, 2 * step : 3 * step], s.mixed2, s.lse2)
    a1 = swap_dp(away_rows(s.n1, dqkv2), size, 1)
    dqkv1 = attend_grad(s.qkv1, s.grad_mixed[:, step : 2 * step], s.mixed1, s.lse1)
    s.put(dqkv1=dqkv1, dqkv2=dqkv2)
    s.add("up0")
    s.add("down0")
    s.drop(low_hidden=0, dy16=0, mixed=0, qkv2=0, mixed2=0, lse2=0, up1=0, down_h=0)
    s.drop(qkv1=0, mixed1=0, lse1=0)
    s.cut()

    def last_half(array):
        return low_half(array), swap_dp(high_half(array), size, far)

    def last_add(kept, arrived):
        return kept.astype(jnp.float32) + arrived.astype(jnp.float32)

    def last_fold(array):
        return last_add(*last_half(array))

    s.put(up0_in=s.up0_x, down0_in=s.down0_y)
    s.add("up0")
    s.add("down0")
    s.send_half("up0", size, near)
    s.send_half("down0", size, near)
    s.send_half("out0", size, 2)
    s.send_half("out1", size, 2)
    a1 = kept_rows(s.n1, s.dqkv2, a1)
    s.put(a0=kept_rows(s.n1, s.dqkv0, a0), a0_in=swap_tensor(a1))
    b0 = swap_dp(away_rows(s.n1, s.dqkv1), size, 1)
    dqkv3 = attend_grad(s.qkv3, s.grad_mixed[:, 3 * step :], s.mixed3, s.lse3)
    b1 = swap_dp(away_rows(s.n1, dqkv3), size, 1)
    s.put(dqkv3=dqkv3)
    s.drop(qkv3=0, mixed3=0, lse3=0, grad_mixed=0, up0_x=0, down0_y=0)
    s.cut()
    for name in ("up0", "down0", "out0", "out1", "a0"):
        s.add(name)
    b1 = kept_rows(s.n1, s.dqkv3, b1)
    s.put(b1=b1)
    s.cut()
    s.put(b0_in=swap_tensor(s.b1), b0=kept_rows(s.n1, s.dqkv1, b0))
    s.send_half("up0", size, far)
    s.send_half("down0", size, far)
    grad_n1 = sum_products(
        [s.dqkv0, s.dqkv1, s.dqkv2, s.dqkv3], [(s.a_own,), (s.b_own,), (s.a_oth,), (s.b_oth,)],
        56 * 2**20,
    )
    s.put(grad_n1=grad_n1)
    s.cut()
    s.put(out0_in=swap_tensor(s.out1))
    s.send_half("a0", size, 2)
    grad_norm, gain_one_grad, bias_one_grad = norm_rows_grad(
        s.grad_n1, s.normal1, s.inverse1, s.gain_one
    )
    rows = reorder((s.grad_hidden + grad_norm).astype(jnp.bfloat16), s.order)
    ours, away = part(rows)
    s.put(input_ours=ours, input_away=away)
    s.put(
        sums=jnp.concatenate(
            [gain_one_grad, bias_one_grad, s.gain_two_grad, s.bias_two_grad], axis=0
        )
    )
    s.drop(grad_n1=0, dqkv0=0, dqkv1=0, dqkv2=0, dqkv3=0, a_own=0, b_own=0, a_oth=0, b_oth=0, out1=0, b1=0)
    s.drop(n1=0, normal1=0, inverse1=0, gain_one=0, grad_hidden=0, order=0)
    s.drop(gain_two_grad=0, bias_two_grad=0)
    s.cut()

    def fold_sums(array, mask):
        middle = array.shape[1] // 2
        return array[:, :middle] + swap_dp(array[:, middle:], size, mask)

    for name in ("b0", "a0", "out0"):
        s.add(name)
    s.send_half("b0", size, 2)
    s.send_half("a0", size, near)
    s.send_half("out0", size, near)
    most = s.input_away.shape[0] // 2
    s.put(most=swap_tensor(s.input_away[:most]), rest=s.input_away[most:])
    s.put(grad_up=last_add(s.up0, s.up0_in), grad_down=last_add(s.down0, s.down0_in))
    s.put(sums=fold_sums(fold_sums(s.sums, 1), 2))
    s.put(block_out=place(s.ours, s.block_arrived))
    s.drop(ours=0, block_arrived=0, input_away=0, up0=0, down0=0, up0_in=0, down0_in=0)
    s.cut()
    for name in ("b0", "a0", "out0"):
        s.add(name)
    s.send_half("b0", size, near)
    s.send_half("a0", size, far)
    s.send_half("out0", size, far)
    s.put(rest=swap_tensor(s.rest), sums=fold_sums(fold_sums(s.sums, near), far))
    s.cut()
    s.add("b0")
    input_grad = place(s.input_ours, jnp.concatenate([s.most, s.rest], axis=0))
    grad_a, grad_out = last_add(s.a0, s.a0_in), last_add(s.out0, s.out0_in)
    grad_b = last_fold(s.b0)
    sums = s.sums + swap_tensor(s.sums)

    return (
        s.block_out,
        input_grad,
        sums[0],
        sums[1],
        jnp.concatenate(
            [g.reshape(row_count, 3, step).transpose(1, 0, 2) for g in (grad_a, grad_b)], axis=2
        ),
        grad_out.T,
        sums[2],
        sums[3],
        s.grad_up,
        s.grad_down.T,
    )


def solution(mesh):
    sizes = dict(mesh.shape)
    dp_size, tensor_size = sizes["dp"], sizes["tensor"]
    if tensor_size == 2 and dp_size == 16:
        body = functools.partial(on_device_whole, dp_size)
    else:
        body = on_device_shared
    placed = (
        P("tensor", "dp", None),
        P("tensor", "dp", None),
        P("dp"),
        P("dp"),
        P(None, "dp", "tensor"),
        P("tensor", "dp"),
        P("dp"),
        P("dp"),
        P("dp", "tensor"),
        P("tensor", "dp"),
    )
    return jax.shard_map(
        body,
        mesh=mesh,
        in_specs=placed,
        out_specs=(
            P("tensor", "dp", None),
            P("tensor", "dp", None),
            P("dp"),
            P("dp"),
            P(None, "dp", "tensor"),
            P("tensor", "dp"),
            P("dp"),
            P("dp"),
            P("dp", "tensor"),
            P("tensor", "dp"),
        ),
        check_vma=False,
    )
```
